32 devices in a mesh: subset: 4 (over y, x), tile: 8 (over z, core).
Axes of the slice: x: 2, y: 2, z: 4, core: 2. Of those that a mesh axis runs over, the one named last changes fastest.
Arguments:
- start_volume: bfloat16 [4, 64, 32768], P(None, None, 'tile'), may hold values from 0 to 2
- measured: bfloat16 [4, 4, 64, 2048], P('subset'), may hold values from 3264 to 13056
- system_values: bfloat16 [4, 2048, 32768], P('subset', None, 'tile'), may hold values from 0.05 to 2088.96, as said below
- block_pattern: int32 [4, 16, 256], P('subset', None, 'tile'), may hold values from 0 to 1, as said below
- subset_order: int32 [64, 4], replicated, may hold values from 0 to 3, each once within a row
Outputs:
- volume_out: bfloat16 [4, 64, 32768], P(None, None, 'tile')
The draws below stay inside these ranges and needn't reach their ends.
Inputs may be any that keep to these rules, and one draw needn't show every extreme that they name: `block_pattern`: each entry is 0 or 1; every block row and every block column of each subset's matrix within every 4096-voxel tile holds at least one 1. `system_values`: positive entries. `subset_order`: each row is a permutation of the 4 subsets.
All inputs are finite; a program needn't handle non-finite values.
Results may differ from the reference program's by a relative error of at most 0.0034.
Values may be sent and summed in bfloat16 or wider, within the bound.
No kernel may reach another device: no remote copies, remote signals or barrier semaphores. Data moves between devices by JAX's collectives and lax.ppermute only.
A program may use at most 128 MiB of HBM per device.

```python
import jax
import jax.numpy as jnp
from jax import lax

TILE_VOX = 4096
SUBSET_RAY_COUNT = 2048
BLOCK_SIDE = 128
SLICES = 64
SWEEP_PASSES = 4
ANGLE_SUBSETS = 4
FRONTS = 4
SLICE_VOX = 32768


def draw_system_values(key, part):
    angle_count = 8
    bins_count = SUBSET_RAY_COUNT // angle_count
    floor_key = jax.random.fold_in(key, 21)
    path_key = jax.random.fold_in(key, 22)
    bin_key = jax.random.fold_in(key, 23)
    floor_part = jax.random.uniform(floor_key, (ANGLE_SUBSETS, angle_count, bins_count, SLICE_VOX), jnp.float32, 0.05, 0.25)
    path_part = jax.random.uniform(path_key, (ANGLE_SUBSETS, angle_count, bins_count, SLICE_VOX), jnp.float32, 0.3, 0.9) * bins_count
    voxel_bins = jax.random.randint(bin_key, (ANGLE_SUBSETS, angle_count, 1, SLICE_VOX), 0, bins_count)
    detector = jnp.arange(bins_count, dtype=jnp.int32)[None, None, :, None]
    values = jnp.where(voxel_bins == detector, path_part, floor_part)
    values = values.reshape(ANGLE_SUBSETS, SUBSET_RAY_COUNT, SLICE_VOX)
    columns = jnp.arange(SLICE_VOX, dtype=jnp.float32) / SLICE_VOX
    ramp = 3.0 ** columns
    return (values * ramp[None, None, :]).astype(jnp.bfloat16)


def draw_block_pattern(key, part):
    blocks_per_row = SUBSET_RAY_COUNT // BLOCK_SIDE
    col_blocks = SLICE_VOX // BLOCK_SIDE
    coins = jax.random.randint(jax.random.fold_in(key, 11), (ANGLE_SUBSETS, blocks_per_row, col_blocks), 0, 100)
    base = (coins < 37).astype(jnp.int32)
    local_cols = jnp.arange(col_blocks, dtype=jnp.int32) % (TILE_VOX // BLOCK_SIDE)
    forced_rows = local_cols % blocks_per_row
    forced = (jnp.arange(blocks_per_row, dtype=jnp.int32)[:, None] == forced_rows[None, :]).astype(jnp.int32)
    return jnp.maximum(base, forced[None, :, :])


def shard_levels(key, shape, cuts, smallest, top_value):
    gain, own = 1.0, jax.random.fold_in(key, 6)
    for dim, blocks in cuts:
        steps = jnp.exp(jax.random.uniform(jax.random.fold_in(own, dim), (blocks,), jnp.float32, smallest / len(cuts), top_value / len(cuts)))
        gain = gain * jnp.repeat(steps, shape[dim] // blocks).reshape([-1 if axis == dim else 1 for axis in range(len(shape))])
    return gain


def setup_inputs(seed: int = 0) -> dict:
    splits = jax.random.split(jax.random.key(seed), 6)
    start_volume = jnp.clip(2.0 * jax.random.uniform(splits[0], (FRONTS, SLICES, SLICE_VOX), jnp.float32) ** shard_levels(splits[0], (FRONTS, SLICES, SLICE_VOX), ((2, 8),), -0.2, 0.2), 0.0, 2.0).astype(jnp.bfloat16)
    measured = jnp.clip(3264.0 + 9792.0 * jax.random.uniform(splits[1], (ANGLE_SUBSETS, FRONTS, SLICES, SUBSET_RAY_COUNT), jnp.float32) ** shard_levels(splits[1], (ANGLE_SUBSETS, FRONTS, SLICES, SUBSET_RAY_COUNT), ((0, 4),), -0.2, 0.2), 3264.0, 13056.0).astype(jnp.bfloat16)
    system_values = draw_system_values(jax.random.fold_in(splits[5], 71), 0)
    block_pattern = draw_block_pattern(jax.random.fold_in(splits[5], 71), 0)
    subset_order = jax.vmap(lambda own: jax.random.permutation(own, ANGLE_SUBSETS))(jax.random.split(splits[4], SLICES)).reshape((SLICES, ANGLE_SUBSETS)).astype(jnp.int32)
    return {"start_volume": start_volume, "measured": measured, "system_values": system_values, "block_pattern": block_pattern, "subset_order": subset_order}


def expand(pattern):
    return jnp.repeat(jnp.repeat(pattern, BLOCK_SIDE, 0), BLOCK_SIDE, 1)


def reference(start_volume, measured, system_values, block_pattern, subset_order):
    volume_all = start_volume.astype(jnp.float32)
    slice_index = jnp.arange(SLICES, dtype=jnp.int32)
    front_index = jnp.arange(FRONTS, dtype=jnp.int32)
    for slice_portion in range(SWEEP_PASSES):
        updated_all = volume_all
        for subset_now in range(ANGLE_SUBSETS):
            hits = ((subset_order + slice_portion) % ANGLE_SUBSETS == subset_now).astype(jnp.int32)
            chosen = jnp.sum(hits * front_index[None, :], axis=1).astype(jnp.int32)
            matrix = system_values[subset_now] * expand(block_pattern[subset_now]).astype(system_values.dtype)
            row_sums = jnp.sum(matrix, axis=1, dtype=jnp.float32)
            column_sums = jnp.sum(matrix, axis=0, dtype=jnp.float32)
            volume = volume_all[chosen, slice_index]
            projected = lax.dot_general(volume.astype(matrix.dtype), matrix, (((1,), (1,)), ((), ())), preferred_element_type=jnp.float32)
            destination_rows = measured[subset_now][chosen, slice_index].astype(jnp.float32)
            residue = ((destination_rows - projected) / row_sums[None, :]).astype(matrix.dtype)
            spread_back = jnp.dot(residue, matrix, preferred_element_type=jnp.float32)
            updated_all = updated_all.at[chosen, slice_index].set(volume + spread_back / column_sums[None, :])
        volume_all = updated_all
    return volume_all.astype(start_volume.dtype)
```

```python
import functools

import jax
import jax.numpy as jnp
from jax import lax
from jax.experimental import pallas as pl
from jax.experimental.pallas import tpu as pltpu
from jax.sharding import PartitionSpec as P

F32, BF16, F16 = jnp.float32, jnp.bfloat16, jnp.float16
RAY_SCALE = 2.0**-14
EXTRA = 16
CHUNKS = 2
LOADS = 8
VM = pl.BlockSpec(memory_space=pltpu.VMEM)
SM = pl.BlockSpec(memory_space=pltpu.SMEM)


def call(kernel, out_shape, args, specs, flops, name, scratch=(), vmem=8 << 20):
    out_specs = jax.tree.map(lambda _: VM, out_shape)
    return pl.pallas_call(
        kernel,
        out_shape=out_shape,
        in_specs=specs,
        out_specs=out_specs,
        scratch_shapes=scratch,
        name=name,
        cost_estimate=pl.CostEstimate(flops=flops, bytes_accessed=flops // 64, transcendentals=0),
        compiler_params=pltpu.CompilerParams(vmem_limit_bytes=vmem),
    )(*args)


def shaped(shape, dtype=F32):
    return jax.ShapeDtypeStruct(shape, dtype)


def dot_nt(a, b):
    return lax.dot_general(a, b, (((1,), (1,)), ((), ())), preferred_element_type=F32)


def dot_nn(a, b):
    return lax.dot_general(a, b, (((1,), (0,)), ((), ())), preferred_element_type=F32)


def load_kernel(matrix_hbm, pattern, volume, matrix, rays, sems):
    ray_blocks, col_blocks = pattern.shape
    ray_count, voxels = matrix.shape
    side = ray_count // ray_blocks
    rows = ray_count // LOADS
    per_load = ray_blocks // LOADS

    def piece(i):
        where = pl.ds(i * rows, rows)
        return pltpu.make_async_copy(matrix_hbm.at[where], matrix.at[where], sems.at[i])

    for i in range(LOADS):
        piece(i).start()

    @pl.loop(0, LOADS)
    def _(i):
        piece(i).wait()
        for r in range(per_load):
            block_row = i * per_load + r
            where = pl.ds(pl.multiple_of(block_row * side, side), side)
            for c in range(col_blocks):
                cols = slice(c * side, (c + 1) * side)
                keep = pattern[block_row, c] != 0
                block = matrix[where, cols]
                matrix[where, cols] = jnp.where(keep, block, jnp.zeros_like(block))
        where = pl.ds(pl.multiple_of(i * rows, rows), rows)
        rays[:, where] = dot_nt(volume[...], matrix[where, :])


def project_first(volume, matrix, rays):
    width = volume.shape[1]
    rays[...] = dot_nt(volume[...], matrix[:, :width])


def project_half(half, volume, so_far, matrix, rays):
    width = volume.shape[1]
    count = rays.shape[1]
    where = pl.ds(pl.multiple_of(half[0] * count, count), count)
    rays[...] = so_far[:, where] + dot_nt(volume[...], matrix[where, matrix.shape[1] - width :])


def spread_first(half, residue, matrix, spread):
    count = residue.shape[1]
    where = pl.ds(pl.multiple_of(half[0] * count, count), count)
    spread[...] = dot_nn(residue[...], matrix[where, :])


def spread_last(chunk, first, half, residue, so_far, volume, column, matrix, out, *column_out):
    count = residue.shape[1]
    slices, width = out.shape
    cols = slice(chunk * width, (chunk + 1) * width)
    where = pl.ds(pl.multiple_of(half[0] * count, count), count)
    total = so_far[:, cols] + dot_nn(residue[...], matrix[where, cols])
    if first:
        inverse = 1.0 / total[slices : slices + 1, :]
        column_out[0][...] = inverse
    else:
        inverse = column[...]
    out[...] = volume[...] + total[:slices] * inverse


def passed(x, axis, distance):
    size = lax.axis_size(axis)
    return lax.ppermute(x, axis, [(i, (i + distance) % size) for i in range(size)])


def swapped(x, axis, bit):
    size = lax.axis_size(axis)
    return lax.ppermute(x, axis, [(i, i ^ bit) for i in range(size)])


def tile_sum(own, received):
    total = own + received.astype(F32)
    bit = 2
    while bit < lax.axis_size("tile"):
        total = total + swapped(total.astype(F16), "tile", bit).astype(F32)
        bit *= 2
    return total


def from_all_owners(chunks):
    owner = lax.axis_index("subset")
    owners = lax.axis_size("subset")
    found = [(owner, chunks)]
    if owners == 4 and len(chunks) == 2:
        near = [swapped(c, "subset", 1) for c in chunks]
        far = [swapped(c, "subset", 2) for c in chunks]
        both = [swapped(far[0], "subset", 1), swapped(near[1], "subset", 2)]
        return found + [(owner ^ 1, near), (owner ^ 2, far), (owner ^ 3, both)]
    for d in range(1, owners):
        found.append(((owner - d) % owners, [passed(c, "subset", d) for c in chunks]))
    return found


def body(start_volume, measured, system_values, block_pattern, subset_order):
    owner = lax.axis_index("subset")
    owners = lax.axis_size("subset")
    core = lax.axis_index("tile") % 2
    own, other = [jnp.reshape(h, (1,)).astype(jnp.int32) for h in (core, 1 - core)]
    fronts, slices, voxels = start_volume.shape
    ray_count = measured.shape[-1]
    half = ray_count // 2
    width = voxels // CHUNKS
    passes = owners

    def mine(j):
        return (subset_order + j) % owners == owner

    def pick(j, parts):
        chosen = mine(j)
        got = parts[0]
        for f in range(1, fronts):
            got = jnp.where(chosen[:, f : f + 1], parts[f], got)
        return got

    start = pick(0, start_volume)
    ones = jnp.ones((EXTRA, voxels), BF16)
    matrix, rays = call(
        load_kernel,
        (pltpu.VMEM((ray_count, voxels), BF16), shaped((slices + EXTRA, ray_count))),
        (system_values[0], block_pattern[0], jnp.concatenate([start, ones])),
        [pl.BlockSpec(memory_space=pltpu.HBM), SM, VM],
        2 * slices * ray_count * voxels,
        "load_and_project",
        scratch=[pltpu.SemaphoreType.DMA((LOADS,))],
    )
    my_rays = lax.dynamic_slice_in_dim(measured[0], core * half, half, 2)
    volume = [start[:, c * width : (c + 1) * width].astype(F32) for c in range(CHUNKS)]
    column = [None] * CHUNKS
    inverse_row = None
    work = 2 * slices * ray_count * voxels
    for j in range(passes):
        if j == 0:
            rest = lax.dynamic_slice_in_dim(rays, (1 - core) * half, half, 1)
            kept = lax.dynamic_slice_in_dim(rays, core * half, half, 1)
        else:
            narrow = [v.astype(BF16) for v in volume]
            so_far = call(
                project_first, shaped((slices, ray_count)), (narrow[0], matrix), [VM, VM],
                work // 2, "project_first",
            )
            rest, kept = [
                call(
                    project_half, shaped((slices, half)), (h, narrow[1], so_far, matrix),
                    [SM, VM, VM, VM], work // 4, "project_half",
                )
                for h in (other, own)
            ]
        received = swapped((rest * RAY_SCALE).astype(F16), "tile", 1)
        total = tile_sum(kept * RAY_SCALE, received)
        if j == 0:
            inverse_row = 1.0 / total[slices : slices + 1]
            total = total[:slices]
        target = pick(j, my_rays).astype(F32) * RAY_SCALE
        residue = ((target - total) * inverse_row).astype(BF16)
        if j == 0:
            residue = jnp.concatenate([residue, jnp.ones((EXTRA, half), BF16)])
        rest_residue = swapped(residue, "tile", 1)
        spread = call(
            spread_first, shaped((residue.shape[0], voxels)), (own, residue, matrix),
            [SM, VM, VM], work // 2, "spread_first",
        )
        for c in range(CHUNKS):
            shapes = [shaped((slices, width))]
            if j == 0:
                shapes.append(shaped((1, width)))
                prior = jnp.zeros((1, width), F32)
            else:
                prior = column[c]
            got = call(
                functools.partial(spread_last, c, j == 0), tuple(shapes),
                (other, rest_residue, spread, volume[c], prior, matrix),
                [SM, VM, VM, VM, VM, VM], work // 4, "spread_last",
            )
            volume[c] = got[0]
            if j == 0:
                column[c] = got[1]
        if j + 1 < passes:
            volume = [passed(v.astype(F16), "subset", 1).astype(F32) for v in volume]

    found = from_all_owners([v.astype(BF16) for v in volume])
    last_owner = jnp.transpose((subset_order + passes - 1) % owners)[:, :, None]
    outs = []
    for c in range(CHUNKS):
        got = jnp.broadcast_to(found[0][1][c][None], (fronts, slices, width))
        for who, chunks in found[1:]:
            got = jnp.where(last_owner == who, chunks[c][None], got)
        outs.append(got)
    return jnp.concatenate(outs, axis=2)


def solution(mesh):
    placed = (
        P(None, None, "tile"),
        P("subset", None, None, None),
        P("subset", None, "tile"),
        P("subset", None, "tile"),
        P(),
    )
    return jax.shard_map(
        body, mesh=mesh, in_specs=placed, out_specs=P(None, None, "tile"), check_vma=False
    )
```

```python
import functools

import jax
import jax.numpy as jnp
from jax import lax
from jax.experimental import pallas as pl
from jax.experimental.pallas import tpu as pltpu
from jax.sharding import PartitionSpec as P

F32, BF16, F16 = jnp.float32, jnp.bfloat16, jnp.float16
RAY_SCALE = 2.0**-14
EXTRA = 16
CHUNKS = 2
GROUPS = 2
VM = pl.BlockSpec(memory_space=pltpu.VMEM)
SM = pl.BlockSpec(memory_space=pltpu.SMEM)
HB = pl.BlockSpec(memory_space=pltpu.HBM)


def call(kernel, out_shape, args, specs, flops, name, scratch=(), vmem=8 << 20):
    out_specs = jax.tree.map(lambda _: VM, out_shape)
    return pl.pallas_call(
        kernel,
        out_shape=out_shape,
        in_specs=specs,
        out_specs=out_specs,
        scratch_shapes=scratch,
        name=name,
        cost_estimate=pl.CostEstimate(flops=flops, bytes_accessed=flops // 64, transcendentals=0),
        compiler_params=pltpu.CompilerParams(vmem_limit_bytes=vmem),
    )(*args)


def shaped(shape, dtype=F32):
    return jax.ShapeDtypeStruct(shape, dtype)


def dot_nt(a, b):
    return lax.dot_general(a, b, (((1,), (1,)), ((), ())), preferred_element_type=F32)


def dot_nn(a, b):
    return lax.dot_general(a, b, (((1,), (0,)), ((), ())), preferred_element_type=F32)


def load_kernel(
    place, matrix_hbm, pattern, order, start_hbm, matrix, narrow, volume, turn, apart, second,
    fronts, sems, start_sem,
):
    ray_blocks, col_blocks = pattern.shape
    ray_count, voxels = matrix.shape
    side = ray_count // ray_blocks
    loads = sems.shape[0]
    rows = ray_count // loads
    per_load = ray_blocks // loads
    slices = fronts.shape[1]
    owner, core, owners = place[0], place[1], place[2]

    def piece(i):
        where = pl.ds(i * rows, rows)
        return pltpu.make_async_copy(matrix_hbm.at[where], matrix.at[where], sems.at[i])

    first = pltpu.make_async_copy(start_hbm, fronts, start_sem)
    first.start()
    for i in range(loads):
        piece(i).start()
    second[...] = jnp.full(second.shape, core.astype(F32))
    later = owner - order[...]
    later = jnp.where(later < 0, later + owners, later)
    turn[...] = later
    last = order[...] + (owners - 1)
    last = jnp.where(last >= owners, last - owners, last)
    apart[...] = last ^ owner
    narrow[slices:, :] = jnp.ones((narrow.shape[0] - slices, voxels), BF16)
    first.wait()
    chosen = [later[:, f : f + 1] == 0 for f in range(1, fronts.shape[0])]
    step = 4 * side

    @pl.loop(0, voxels // step)
    def _(i):
        cols = pl.ds(pl.multiple_of(i * step, step), step)
        got = fronts[0, :, cols].astype(F32)
        for f, here in enumerate(chosen):
            got = jnp.where(here, fronts[f + 1, :, cols].astype(F32), got)
        volume[:, cols] = got
        narrow[:slices, cols] = got.astype(BF16)

    @pl.loop(0, loads)
    def _(i):
        piece(i).wait()
        for r in range(per_load):
            block_row = i * per_load + r
            where = pl.ds(pl.multiple_of(block_row * side, side), side)
            for c in range(col_blocks):

                @pl.when(pattern[block_row, c] == 0)
                def _():
                    matrix[where, c * side : (c + 1) * side] = jnp.zeros((side, side), BF16)


def project_first(chunk, volume, matrix, rays):
    width = volume.shape[1]
    rays[...] = dot_nt(volume[...], matrix[:, chunk * width : (chunk + 1) * width])


def project_next(chunk, volume, so_far, matrix, rays):
    width = volume.shape[1]
    rays[...] = so_far[...] + dot_nt(volume[...], matrix[:, chunk * width : (chunk + 1) * width])


def project_whole(place, volume, matrix, rays):
    count = rays.shape[1]
    where = pl.ds(pl.multiple_of(place[0] * count, count), count)
    rays[...] = dot_nt(volume[...], matrix[where, :])


def project_piece(place, volume, so_far, matrix, rays):
    width = volume.shape[1]
    count = rays.shape[1]
    where = pl.ds(pl.multiple_of(place[0] * count, count), count)
    rays[...] = so_far[:, where] + dot_nt(volume[...], matrix[where, matrix.shape[1] - width :])


def spread_pair(mine, theirs, residue, their_residue, matrix, spread):
    count = residue.shape[1]
    where = pl.ds(pl.multiple_of(mine[0] * count, count), count)
    also = pl.ds(pl.multiple_of(theirs[0] * count, count), count)
    step = matrix.shape[1] // 4
    for c in range(4):
        cols = slice(c * step, (c + 1) * step)
        spread[:, cols] = dot_nn(residue[...], matrix[where, cols]) + dot_nn(
            their_residue[...], matrix[also, cols]
        )


def spread_next(place, residue, so_far, matrix, spread):
    count = residue.shape[1]
    where = pl.ds(pl.multiple_of(place[0] * count, count), count)
    step = matrix.shape[1] // 4
    for c in range(4):
        cols = slice(c * step, (c + 1) * step)
        spread[:, cols] = so_far[:, cols] + dot_nn(residue[...], matrix[where, cols])


def spread_last(chunk, first, place, residue, so_far, volume, column, matrix, out, *column_out):
    count = residue.shape[1]
    slices, width = out.shape
    cols = slice(chunk * width, (chunk + 1) * width)
    where = pl.ds(pl.multiple_of(place[0] * count, count), count)
    total = so_far[:, cols] + dot_nn(residue[...], matrix[where, cols])
    if first:
        inverse = 1.0 / total[slices : slices + 1, :]
        column_out[0][...] = inverse
        prior = volume[:, cols]
    else:
        inverse = column[...]
        prior = volume[...]
    out[...] = prior + total[:slices] * inverse


def passed(x, axis, distance):
    size = lax.axis_size(axis)
    return lax.ppermute(x, axis, [(i, (i + distance) % size) for i in range(size)])


def swapped(x, axis, bit):
    size = lax.axis_size(axis)
    return lax.ppermute(x, axis, [(i, i ^ bit) for i in range(size)])


def tile_sum(own, received):
    total = own + received.astype(F32)
    bit = 2
    while bit < lax.axis_size("tile"):
        total = total + swapped(total.astype(F16), "tile", bit).astype(F32)
        bit *= 2
    return total


def from_all_owners(chunks):
    owners = lax.axis_size("subset")
    if owners == 4 and len(chunks) == 2:
        near = [swapped(c, "subset", 1) for c in chunks]
        far = [swapped(c, "subset", 2) for c in chunks]
        both = [swapped(far[0], "subset", 1), swapped(near[1], "subset", 2)]
        return [chunks, near, far, both]
    return [chunks] + [[swapped(c, "subset", d) for c in chunks] for d in range(1, owners)]


def body(start_volume, measured, system_values, block_pattern, subset_order):
    owner = lax.axis_index("subset")
    owners = lax.axis_size("subset")
    core = lax.axis_index("tile") % 2
    fronts, slices, voxels = start_volume.shape
    ray_count = measured.shape[-1]
    ray_blocks = block_pattern.shape[1]
    piece = ray_count // (2 * GROUPS)
    width = voxels // CHUNKS
    passes = owners
    loads = ray_blocks // 2
    work = 2 * slices * ray_count * voxels
    place = jnp.stack([owner, core, jnp.int32(owners)]).astype(jnp.int32)
    own = [jnp.reshape(2 * g + core, (1,)).astype(jnp.int32) for g in range(GROUPS)]
    other = [jnp.reshape(2 * g + 1 - core, (1,)).astype(jnp.int32) for g in range(GROUPS)]
    place, own, other = lax.optimization_barrier((place, own, other))
    rows = slices + EXTRA

    def pick(j, parts):
        got = parts[0]
        for f in range(1, fronts):
            got = jnp.where(turn[:, f : f + 1] == j, parts[f], got)
        return got

    hbm = pltpu.with_memory_space_constraint
    matrix, all_rows, volume, turn, apart, second = call(
        load_kernel,
        (
            pltpu.VMEM((ray_count, voxels), BF16),
            shaped((rows, voxels), BF16),
            shaped((slices, voxels)),
            shaped((slices, fronts), jnp.int32),
            shaped((slices, fronts), jnp.int32),
            shaped((1, piece)),
        ),
        (
            place, hbm(system_values[0], pltpu.HBM), block_pattern[0], subset_order,
            hbm(start_volume, pltpu.HBM),
        ),
        [SM, HB, SM, VM, HB],
        work,
        "load",
        scratch=[
            pltpu.VMEM((fronts, slices, voxels), BF16),
            pltpu.SemaphoreType.DMA((loads,)),
            pltpu.SemaphoreType.DMA,
        ],
        vmem=10 << 20,
    )
    matrix = pltpu.with_memory_space_constraint(matrix, pltpu.VMEM)
    volume = [volume] * CHUNKS
    column = [None] * CHUNKS
    inverse_row = [None] * GROUPS
    for j in range(passes):
        if j == 0:

            def project(where):
                return call(
                    project_whole, shaped((rows, piece)), (where, all_rows, matrix),
                    [SM, VM, VM], work // (2 * GROUPS), "project_whole",
                )

        else:
            narrow = [v.astype(BF16) for v in volume]
            so_far = call(
                functools.partial(project_first, 0), shaped((slices, ray_count)),
                (narrow[0], matrix), [VM, VM], work // CHUNKS, "project_first",
            )
            for c in range(1, CHUNKS - 1):
                so_far = call(
                    functools.partial(project_next, c), shaped((slices, ray_count)),
                    (narrow[c], so_far, matrix), [VM, VM, VM], work // CHUNKS, "project_next",
                )

            def project(where):
                return call(
                    project_piece, shaped((slices, piece)), (where, narrow[-1], so_far, matrix),
                    [SM, VM, VM, VM], work // (CHUNKS * 2 * GROUPS), "project_piece",
                )

        targets = [
            measured[0][:, :, 2 * g * piece : (2 * g + 2) * piece] for g in range(GROUPS)
        ]
        targets = [
            jnp.where(second == 0, t[:, :, :piece], t[:, :, piece:]).astype(F32) for t in targets
        ]
        residues = []
        for g in range(GROUPS):
            sent = project(other[g])
            received = swapped((sent * RAY_SCALE).astype(F16), "tile", 1)
            held = project(own[g])
            total = tile_sum(held * RAY_SCALE, received)
            if j == 0:
                inverse_row[g] = 1.0 / total[slices : slices + 1]
                total = total[:slices]
            target = pick(j, targets[g]) * RAY_SCALE
            residue = ((target - total) * inverse_row[g]).astype(BF16)
            if j == 0:
                residue = jnp.concatenate([residue, jnp.ones((EXTRA, piece), BF16)])
            residues.append((residue, swapped(residue, "tile", 1)))
        height = residues[0][0].shape[0]
        for g in range(GROUPS - 1):
            if g == 0:
                spread = call(
                    spread_pair, shaped((height, voxels)),
                    (own[g], other[g], *residues[g], matrix), [SM, SM, VM, VM, VM],
                    work // GROUPS, "spread_pair",
                )
        spread = call(
            spread_next, shaped((height, voxels)), (own[-1], residues[-1][0], spread, matrix),
            [SM, VM, VM, VM], work // (2 * GROUPS), "spread_next",
        )
        for c in range(CHUNKS):
            shapes = [shaped((slices, width))]
            if j == 0:
                shapes.append(shaped((1, width)))
                prior = jnp.zeros((1, width), F32)
            else:
                prior = column[c]
            got = call(
                functools.partial(spread_last, c, j == 0), tuple(shapes),
                (other[-1], residues[-1][1], spread, volume[c], prior, matrix),
                [SM, VM, VM, VM, VM, VM], work // (2 * GROUPS * CHUNKS), "spread_last",
            )
            volume[c] = got[0]
            if j == 0:
                column[c] = got[1]
        if j + 1 < passes:
            volume = [passed(v.astype(F16), "subset", 1).astype(F32) for v in volume]

    found = from_all_owners([v.astype(BF16) for v in volume])
    outs = []
    for f in range(fronts):
        parts = []
        for c in range(CHUNKS):
            got = found[0][c]
            for d in range(1, owners):
                got = jnp.where(apart[:, f : f + 1] == d, found[d][c], got)
            parts.append(got)
        outs.append(jnp.concatenate(parts, axis=1))
    return jnp.stack(outs)


def solution(mesh):
    placed = (
        P(None, None, "tile"),
        P("subset", None, None, None),
        P("subset", None, "tile"),
        P("subset", None, "tile"),
        P(),
    )
    return jax.shard_map(
        body, mesh=mesh, in_specs=placed, out_specs=P(None, None, "tile"), check_vma=False
    )
```

```python
import functools

import jax
import jax.numpy as jnp
from jax import lax
from jax.experimental import pallas as pl
from jax.experimental.pallas import tpu as pltpu
from jax.sharding import PartitionSpec as P

F32, BF16, F16 = jnp.float32, jnp.bfloat16, jnp.float16
RAY_SCALE = 2.0**-14
EXTRA = 16
COST = 16
AHEAD = 2
BATCHES = 2
VM = pl.BlockSpec(memory_space=pltpu.VMEM)
SM = pl.BlockSpec(memory_space=pltpu.SMEM)
HB = pl.BlockSpec(memory_space=pltpu.HBM)


def call(kernel, out_shape, args, specs, flops, name, scratch=(), vmem=8 << 20):
    out_specs = jax.tree.map(lambda _: VM, out_shape)
    return pl.pallas_call(
        kernel,
        out_shape=out_shape,
        in_specs=specs,
        out_specs=out_specs,
        scratch_shapes=scratch,
        name=name,
        cost_estimate=pl.CostEstimate(
            flops=COST * flops, bytes_accessed=0, transcendentals=0
        ),
        compiler_params=pltpu.CompilerParams(vmem_limit_bytes=vmem),
    )(*args)


def shaped(shape, dtype=F32):
    return jax.ShapeDtypeStruct(shape, dtype)


def dot_nn(a, b):
    return lax.dot_general(a, b, (((1,), (0,)), ((), ())), preferred_element_type=F32)


def load_kernel(
    place, matrix_hbm, pattern, order, start_hbm, matrix, flipped, narrow, volume, turn, apart,
    second, fronts, sems, start_sem,
):
    ray_blocks, col_blocks = pattern.shape
    ray_count, voxels = matrix.shape
    side = ray_count // ray_blocks
    loads = sems.shape[0]
    rows = ray_count // loads
    per_load = ray_blocks // loads
    slices = fronts.shape[1]
    owner, core, owners = place[0], place[1], place[2]

    def piece(i):
        where = pl.ds(pl.multiple_of(i * rows, rows), rows)
        return pltpu.make_async_copy(matrix_hbm.at[where], matrix.at[where], sems.at[i])

    first = pltpu.make_async_copy(start_hbm, fronts, start_sem)
    first.start()
    for i in range(AHEAD):
        piece(i).start()
    second[...] = jnp.full(second.shape, core.astype(F32))
    later = owner - order[...]
    later = jnp.where(later < 0, later + owners, later)
    turn[...] = later
    last = order[...] + (owners - 1)
    last = jnp.where(last >= owners, last - owners, last)
    apart[...] = last ^ owner
    batches, rows_in = narrow.shape[:2]
    batch = slices // batches
    narrow[:, batch:, :] = jnp.ones((batches, rows_in - batch, voxels), BF16)
    first.wait()
    chosen = [later[:, f : f + 1] == 0 for f in range(1, fronts.shape[0])]
    step = 4 * side

    @pl.loop(0, voxels // step)
    def _(i):
        cols = pl.ds(pl.multiple_of(i * step, step), step)
        got = fronts[0, :, cols].astype(F32)
        for f, here in enumerate(chosen):
            got = jnp.where(here, fronts[f + 1, :, cols].astype(F32), got)
        for b in range(batches):
            part = got[b * batch : (b + 1) * batch]
            volume[b, :, cols] = part
            narrow[b, :batch, cols] = part.astype(BF16)

    @pl.loop(0, loads)
    def _(i):
        piece(i).wait()

        @pl.when(i + AHEAD < loads)
        def _():
            piece(i + AHEAD).start()

        where = pl.ds(pl.multiple_of(i * rows, rows), rows)
        for c in range(0, col_blocks, 2):
            cols = slice(c * side, (c + 2) * side)
            blocks = matrix[where, cols]
            masked = []
            for r in range(per_load):
                keep = [pattern[i * per_load + r, c + k].astype(F32).astype(BF16) for k in (0, 1)]
                part = blocks[r * side : (r + 1) * side]
                masked.append(
                    jnp.concatenate([part[:, :side] * keep[0], part[:, side:] * keep[1]], 1)
                )
            blocks = jnp.concatenate(masked, 0)
            matrix[where, cols] = blocks
            flipped[cols, where] = blocks.T


def project(place, volume, flipped, rays):
    count = rays.shape[1]
    where = pl.ds(pl.multiple_of(place[0] * count, count), count)
    rays[...] = dot_nn(volume[...], flipped[:, where])


def spread_first(place, residue, matrix, spread):
    count = residue.shape[1]
    where = pl.ds(pl.multiple_of(place[0] * count, count), count)
    step = matrix.shape[1] // 4
    for c in range(4):
        cols = slice(c * step, (c + 1) * step)
        spread[:, cols] = dot_nn(residue[...], matrix[where, cols])


def spread_last(first, place, residue, so_far, volume, column, matrix, out, *column_out):
    count = residue.shape[1]
    slices = out.shape[0]
    step = matrix.shape[1] // 4
    where = pl.ds(pl.multiple_of(place[0] * count, count), count)
    for c in range(4):
        cols = slice(c * step, (c + 1) * step)
        total = so_far[:, cols] + dot_nn(residue[...], matrix[where, cols])
        if first:
            inverse = 1.0 / total[slices : slices + 1, :]
            column_out[0][:, cols] = inverse
        else:
            inverse = column[:, cols]
        out[:, cols] = volume[:, cols] + total[:slices] * inverse


def passed(x, axis, distance):
    size = lax.axis_size(axis)
    return lax.ppermute(x, axis, [(i, (i + distance) % size) for i in range(size)])


def swapped(x, axis, bit):
    size = lax.axis_size(axis)
    return lax.ppermute(x, axis, [(i, i ^ bit) for i in range(size)])


def after(value, token):
    return value if token is None else lax.optimization_barrier((value, token))[0]


def from_all_owners(block):
    owners = lax.axis_size("subset")
    if owners != 4:
        return [block] + [swapped(block, "subset", d) for d in range(1, owners)]
    half = block.shape[1] // 2
    near = swapped(block, "subset", 1)
    far = swapped(block, "subset", 2)
    both = [swapped(far[:, :half], "subset", 1), swapped(near[:, half:], "subset", 2)]
    return [block, near, far, jnp.concatenate(both, axis=1)]


def body(start_volume, measured, system_values, block_pattern, subset_order):
    owner = lax.axis_index("subset")
    owners = lax.axis_size("subset")
    core = lax.axis_index("tile") % 2
    tiles = lax.axis_size("tile")
    fronts, slices, voxels = start_volume.shape
    ray_count = measured.shape[-1]
    ray_blocks = block_pattern.shape[1]
    half = ray_count // 2
    batch = slices // BATCHES
    rows = batch + EXTRA
    passes = owners
    loads = ray_blocks // 2
    work = 2 * slices * ray_count * voxels
    place = jnp.stack([owner, core, jnp.int32(owners)]).astype(jnp.int32)
    own = jnp.reshape(core, (1,)).astype(jnp.int32)
    other = jnp.reshape(1 - core, (1,)).astype(jnp.int32)
    place, own, other = lax.optimization_barrier((place, own, other))

    def pick(turns, j, parts):
        got = parts[0]
        for f in range(1, fronts):
            got = jnp.where(turns[:, f : f + 1] == j, parts[f], got)
        return got

    hbm = pltpu.with_memory_space_constraint
    matrix, flipped, all_rows, volume, turn, apart, second = call(
        load_kernel,
        (
            pltpu.VMEM((ray_count, voxels), BF16),
            pltpu.VMEM((voxels, ray_count), BF16),
            shaped((BATCHES, rows, voxels), BF16),
            shaped((BATCHES, batch, voxels)),
            shaped((slices, fronts), jnp.int32),
            shaped((slices, fronts), jnp.int32),
            shaped((1, half)),
        ),
        (
            place, hbm(system_values[0], pltpu.HBM), block_pattern[0], subset_order,
            hbm(start_volume, pltpu.HBM),
        ),
        [SM, HB, SM, VM, HB],
        work,
        "load",
        scratch=[
            pltpu.VMEM((fronts, slices, voxels), BF16),
            pltpu.SemaphoreType.DMA((loads,)),
            pltpu.SemaphoreType.DMA,
        ],
        vmem=10 << 20,
    )
    matrix = pltpu.with_memory_space_constraint(matrix, pltpu.VMEM)
    flipped = pltpu.with_memory_space_constraint(flipped, pltpu.VMEM)

    def products(kernel, shape, args, specs, name):
        return call(kernel, shape, args, specs, work // 2, name)

    targets = jnp.where(second == 0, measured[0][:, :, :half], measured[0][:, :, half:])
    these = [slice(n * batch, (n + 1) * batch) for n in range(BATCHES)]
    now = [volume[n] for n in range(BATCHES)]
    narrow = [all_rows[n] for n in range(BATCHES)]
    column = [jnp.zeros((1, voxels), F32)] * BATCHES
    inverse_row = [None] * BATCHES
    token = None
    for j in range(passes):
        totals = []
        for n in range(BATCHES):
            if j > 0:
                now[n] = after(now[n], token).astype(F32)
                narrow[n] = now[n].astype(BF16)
            height = narrow[n].shape[0]
            sent, held = [
                products(
                    project, shaped((height, half)), (where, narrow[n], flipped), [SM, VM, VM],
                    "project",
                )
                for where in (other, own)
            ]
            got = swapped((sent * RAY_SCALE).astype(F16), "tile", 1)
            totals.append(held * RAY_SCALE + got.astype(F32))
            token = totals[n].astype(F16)
        bit = 2
        while bit < tiles:
            got = [swapped(t.astype(F16), "tile", bit) for t in totals]
            for n in range(BATCHES):
                totals[n] = totals[n] + after(got[n], token).astype(F32)
                token = totals[n].astype(F16)
            bit *= 2
        for n in range(BATCHES):
            total = totals[n] if n == 0 else after(totals[n], token)
            if j == 0:
                inverse_row[n] = 1.0 / total[batch : batch + 1]
                total = total[:batch]
            target = pick(turn[these[n]], j, targets[:, these[n]].astype(F32)) * RAY_SCALE
            residue = ((target - total) * inverse_row[n]).astype(BF16)
            if j == 0:
                residue = jnp.concatenate([residue, jnp.ones((EXTRA, half), BF16)])
            height = residue.shape[0]
            their_residue = swapped(residue, "tile", 1)
            spread = products(
                spread_first, shaped((height, voxels)), (own, residue, matrix),
                [SM, VM, VM], "spread_first",
            )
            shapes = [shaped((batch, voxels))]
            if j == 0:
                shapes.append(shaped((1, voxels)))
            got = products(
                functools.partial(spread_last, j == 0), tuple(shapes),
                (other, their_residue, spread, now[n], column[n], matrix),
                [SM, VM, VM, VM, VM, VM], "spread_last",
            )
            now[n] = got[0]
            if j == 0:
                column[n] = got[1]
            token = now[n].astype(F16)
            if j + 1 < passes:
                now[n] = passed(token, "subset", 1)
    outs = []
    for n in range(BATCHES):
        found = from_all_owners(now[n].astype(BF16))
        parts = []
        for f in range(fronts):
            got = found[0]
            for d in range(1, owners):
                got = jnp.where(apart[these[n], f : f + 1] == d, found[d], got)
            parts.append(got)
        outs.append(jnp.stack(parts))
    return jnp.concatenate(outs, axis=1)


def solution(mesh):
    placed = (
        P(None, None, "tile"),
        P("subset", None, None, None),
        P("subset", None, "tile"),
        P("subset", None, "tile"),
        P(),
    )
    return jax.shard_map(
        body, mesh=mesh, in_specs=placed, out_specs=P(None, None, "tile"), check_vma=False
    )
```

```python
import functools

import jax
import jax.numpy as jnp
from jax import lax
from jax.experimental import pallas as pl
from jax.experimental.pallas import tpu as pltpu
from jax.sharding import PartitionSpec as P

F32, BF16, F16 = jnp.float32, jnp.bfloat16, jnp.float16
RAY_SCALE = 2.0**-14
EXTRA = 16
COST = 16
AHEAD = 2
BATCHES = 2
VM = pl.BlockSpec(memory_space=pltpu.VMEM)
SM = pl.BlockSpec(memory_space=pltpu.SMEM)
HB = pl.BlockSpec(memory_space=pltpu.HBM)


def call(kernel, out_shape, args, specs, flops, name, scratch=(), vmem=8 << 20):
    out_specs = jax.tree.map(lambda _: VM, out_shape)
    return pl.pallas_call(
        kernel,
        out_shape=out_shape,
        in_specs=specs,
        out_specs=out_specs,
        scratch_shapes=scratch,
        name=name,
        cost_estimate=pl.CostEstimate(
            flops=COST * flops, bytes_accessed=0, transcendentals=0
        ),
        compiler_params=pltpu.CompilerParams(vmem_limit_bytes=vmem),
    )(*args)


def shaped(shape, dtype=F32):
    return jax.ShapeDtypeStruct(shape, dtype)


def dot_nn(a, b):
    return lax.dot_general(a, b, (((1,), (0,)), ((), ())), preferred_element_type=F32)


def load_kernel(
    place, matrix_hbm, pattern, order, start_hbm, matrix, flipped, narrow, volume, turn, apart,
    second, fronts, sems, start_sem,
):
    ray_blocks, col_blocks = pattern.shape
    ray_count, voxels = matrix.shape
    side = ray_count // ray_blocks
    loads = sems.shape[0]
    rows = ray_count // loads
    per_load = ray_blocks // loads
    slices = fronts.shape[1]
    owner, core, owners = place[0], place[1], place[2]

    def piece(i):
        where = pl.ds(pl.multiple_of(i * rows, rows), rows)
        return pltpu.make_async_copy(matrix_hbm.at[where], matrix.at[where], sems.at[i])

    first = pltpu.make_async_copy(start_hbm, fronts, start_sem)
    first.start()
    for i in range(AHEAD):
        piece(i).start()
    second[...] = jnp.full(second.shape, core.astype(F32))
    later = owner - order[...]
    later = jnp.where(later < 0, later + owners, later)
    turn[...] = later
    last = order[...] + (owners - 1)
    last = jnp.where(last >= owners, last - owners, last)
    apart[...] = last ^ owner
    batches, rows_in = narrow.shape[:2]
    batch = slices // batches
    narrow[:, batch:, :] = jnp.ones((batches, rows_in - batch, voxels), BF16)
    first.wait()
    chosen = [later[:, f : f + 1] == 0 for f in range(1, fronts.shape[0])]
    step = 4 * side

    @pl.loop(0, voxels // step)
    def _(i):
        cols = pl.ds(pl.multiple_of(i * step, step), step)
        got = fronts[0, :, cols].astype(F32)
        for f, here in enumerate(chosen):
            got = jnp.where(here, fronts[f + 1, :, cols].astype(F32), got)
        for b in range(batches):
            part = got[b * batch : (b + 1) * batch]
            volume[b, :, cols] = part
            narrow[b, :batch, cols] = part.astype(BF16)

    @pl.loop(0, loads)
    def _(i):
        piece(i).wait()

        @pl.when(i + AHEAD < loads)
        def _():
            piece(i + AHEAD).start()

        where = pl.ds(pl.multiple_of(i * rows, rows), rows)
        for c in range(0, col_blocks, 2):
            cols = slice(c * side, (c + 2) * side)
            blocks = matrix[where, cols]
            masked = []
            for r in range(per_load):
                keep = [pattern[i * per_load + r, c + k].astype(F32).astype(BF16) for k in (0, 1)]
                part = blocks[r * side : (r + 1) * side]
                masked.append(
                    jnp.concatenate([part[:, :side] * keep[0], part[:, side:] * keep[1]], 1)
                )
            blocks = jnp.concatenate(masked, 0)
            matrix[where, cols] = blocks
            flipped[cols, where] = blocks.T


def project(place, volume, flipped, rays):
    count = rays.shape[1]
    step = min(count, 1024)
    offset = place[0] * count

    @pl.loop(0, count // step)
    def _(i):
        where = pl.ds(pl.multiple_of(offset + i * step, step), step)
        rays[:, pl.ds(pl.multiple_of(i * step, step), step)] = dot_nn(volume[...], flipped[:, where])


def spread_first(place, residue, matrix, spread):
    count = residue.shape[1]
    where = pl.ds(pl.multiple_of(place[0] * count, count), count)
    step = 2048

    @pl.loop(0, matrix.shape[1] // step)
    def _(c):
        cols = pl.ds(pl.multiple_of(c * step, step), step)
        spread[:, cols] = dot_nn(residue[...], matrix[where, cols])


def spread_last(first, place, residue, so_far, volume, column, matrix, out, *column_out):
    count = residue.shape[1]
    slices = out.shape[0]
    step = 2048
    where = pl.ds(pl.multiple_of(place[0] * count, count), count)

    @pl.loop(0, matrix.shape[1] // step)
    def _(c):
        cols = pl.ds(pl.multiple_of(c * step, step), step)
        total = so_far[:, cols] + dot_nn(residue[...], matrix[where, cols])
        if first:
            inverse = 1.0 / total[slices : slices + 1, :]
            column_out[0][:, cols] = inverse
        else:
            inverse = column[:, cols]
        out[:, cols] = volume[:, cols] + total[:slices] * inverse


def passed(x, axis, distance):
    size = lax.axis_size(axis)
    return lax.ppermute(x, axis, [(i, (i + distance) % size) for i in range(size)])


def swapped(x, axis, bit):
    size = lax.axis_size(axis)
    return lax.ppermute(x, axis, [(i, i ^ bit) for i in range(size)])


def after(value, token):
    return value if token is None else lax.optimization_barrier((value, token))[0]


def from_all_owners(block):
    owners = lax.axis_size("subset")
    if owners != 4:
        return [block] + [swapped(block, "subset", d) for d in range(1, owners)]
    half = block.shape[1] // 2
    near = swapped(block, "subset", 1)
    far = swapped(block, "subset", 2)
    both = [swapped(far[:, :half], "subset", 1), swapped(near[:, half:], "subset", 2)]
    return [block, near, far, jnp.concatenate(both, axis=1)]


def body(start_volume, measured, system_values, block_pattern, subset_order):
    owner = lax.axis_index("subset")
    owners = lax.axis_size("subset")
    core = lax.axis_index("tile") % 2
    tiles = lax.axis_size("tile")
    fronts, slices, voxels = start_volume.shape
    ray_count = measured.shape[-1]
    ray_blocks = block_pattern.shape[1]
    half = ray_count // 2
    batch = slices // BATCHES
    rows = batch + EXTRA
    passes = owners
    loads = ray_blocks // 2
    work = 2 * slices * ray_count * voxels
    place = jnp.stack([owner, core, jnp.int32(owners)]).astype(jnp.int32)
    own = jnp.reshape(core, (1,)).astype(jnp.int32)
    other = jnp.reshape(1 - core, (1,)).astype(jnp.int32)
    place, own, other = lax.optimization_barrier((place, own, other))

    def pick(turns, j, parts):
        got = parts[0]
        for f in range(1, fronts):
            got = jnp.where(turns[:, f : f + 1] == j, parts[f], got)
        return got

    hbm = pltpu.with_memory_space_constraint
    matrix, flipped, all_rows, volume, turn, apart, second = call(
        load_kernel,
        (
            pltpu.VMEM((ray_count, voxels), BF16),
            pltpu.VMEM((voxels, ray_count), BF16),
            shaped((BATCHES, rows, voxels), BF16),
            shaped((BATCHES, batch, voxels)),
            shaped((slices, fronts), jnp.int32),
            shaped((slices, fronts), jnp.int32),
            shaped((1, half)),
        ),
        (
            place, hbm(system_values[0], pltpu.HBM), block_pattern[0], subset_order,
            hbm(start_volume, pltpu.HBM),
        ),
        [SM, HB, SM, VM, HB],
        work,
        "load",
        scratch=[
            pltpu.VMEM((fronts, slices, voxels), BF16),
            pltpu.SemaphoreType.DMA((loads,)),
            pltpu.SemaphoreType.DMA,
        ],
        vmem=10 << 20,
    )
    matrix = pltpu.with_memory_space_constraint(matrix, pltpu.VMEM)
    flipped = pltpu.with_memory_space_constraint(flipped, pltpu.VMEM)

    def products(kernel, shape, args, specs, name):
        return call(kernel, shape, args, specs, work // 2, name)

    targets = jnp.where(second == 0, measured[0][:, :, :half], measured[0][:, :, half:])
    these = [slice(n * batch, (n + 1) * batch) for n in range(BATCHES)]
    now = [volume[n] for n in range(BATCHES)]
    narrow = [all_rows[n] for n in range(BATCHES)]
    column = [jnp.zeros((1, voxels), F32)] * BATCHES
    inverse_row = [None] * BATCHES
    token = None
    for j in range(passes):
        totals = []
        for n in range(BATCHES):
            if j > 0:
                now[n] = after(now[n], token).astype(F32)
                narrow[n] = now[n].astype(BF16)
            height = narrow[n].shape[0]
            sent, held = [
                products(
                    project, shaped((height, half)), (where, narrow[n], flipped), [SM, VM, VM],
                    "project",
                )
                for where in (other, own)
            ]
            got = swapped((sent * RAY_SCALE).astype(F16), "tile", 1)
            totals.append(held * RAY_SCALE + got.astype(F32))
            token = totals[n].astype(F16)
        bit = 2
        while bit < tiles:
            got = [swapped(t.astype(F16), "tile", bit) for t in totals]
            for n in range(BATCHES):
                totals[n] = totals[n] + after(got[n], token).astype(F32)
                token = totals[n].astype(F16)
            bit *= 2
        for n in range(BATCHES):
            total = totals[n] if n == 0 else after(totals[n], token)
            if j == 0:
                inverse_row[n] = 1.0 / total[batch : batch + 1]
                total = total[:batch]
            target = pick(turn[these[n]], j, targets[:, these[n]].astype(F32)) * RAY_SCALE
            residue = ((target - total) * inverse_row[n]).astype(BF16)
            if j == 0:
                residue = jnp.concatenate([residue, jnp.ones((EXTRA, half), BF16)])
            height = residue.shape[0]
            their_residue = swapped(residue, "tile", 1)
            spread = products(
                spread_first, shaped((height, voxels)), (own, residue, matrix),
                [SM, VM, VM], "spread_first",
            )
            shapes = [shaped((batch, voxels))]
            if j == 0:
                shapes.append(shaped((1, voxels)))
            got = products(
                functools.partial(spread_last, j == 0), tuple(shapes),
                (other, their_residue, spread, now[n], column[n], matrix),
                [SM, VM, VM, VM, VM, VM], "spread_last",
            )
            now[n] = got[0]
            if j == 0:
                column[n] = got[1]
            token = now[n].astype(F16)
            if j + 1 < passes:
                now[n] = passed(token, "subset", 1)
    outs = []
    for n in range(BATCHES):
        found = from_all_owners(now[n].astype(BF16))
        parts = []
        for f in range(fronts):
            got = found[0]
            for d in range(1, owners):
                got = jnp.where(apart[these[n], f : f + 1] == d, found[d], got)
            parts.append(got)
        outs.append(jnp.stack(parts))
    return jnp.concatenate(outs, axis=1)


def solution(mesh):
    placed = (
        P(None, None, "tile"),
        P("subset", None, None, None),
        P("subset", None, "tile"),
        P("subset", None, "tile"),
        P(),
    )
    return jax.shard_map(
        body, mesh=mesh, in_specs=placed, out_specs=P(None, None, "tile"), check_vma=False
    )
```

```python
import functools

import jax
import jax.numpy as jnp
from jax import lax
from jax.experimental import pallas as pl
from jax.experimental.pallas import tpu as pltpu
from jax.sharding import PartitionSpec as P

F32, BF16, F16 = jnp.float32, jnp.bfloat16, jnp.float16
RAY_SCALE = 2.0**-14
EXTRA = 16
COST = 16
AHEAD = 3
BATCHES = 2
VM = pl.BlockSpec(memory_space=pltpu.VMEM)
SM = pl.BlockSpec(memory_space=pltpu.SMEM)
HB = pl.BlockSpec(memory_space=pltpu.HBM)
AN = pl.BlockSpec(memory_space=pl.ANY)


def call(kernel, out_shape, args, specs, flops, name, scratch=(), vmem=8 << 20):
    out_specs = jax.tree.map(lambda _: VM, out_shape)
    return pl.pallas_call(
        kernel,
        out_shape=out_shape,
        in_specs=specs,
        out_specs=out_specs,
        scratch_shapes=scratch,
        name=name,
        cost_estimate=pl.CostEstimate(
            flops=COST * flops, bytes_accessed=0, transcendentals=0
        ),
        compiler_params=pltpu.CompilerParams(vmem_limit_bytes=vmem),
    )(*args)


def shaped(shape, dtype=F32):
    return jax.ShapeDtypeStruct(shape, dtype)


def dot_nn(a, b):
    return lax.dot_general(a, b, (((1,), (0,)), ((), ())), preferred_element_type=F32)


def load_kernel(
    place, matrix_hbm, pattern_hbm, order, start_hbm, matrix, flipped, narrow, volume, turn, apart,
    second, fronts, pattern, sems, start_sem, pattern_sem,
):
    ray_blocks, col_blocks = pattern.shape
    ray_count, voxels = matrix.shape
    side = ray_count // ray_blocks
    loads = sems.shape[0]
    rows = ray_count // loads
    per_load = ray_blocks // loads
    slices = fronts.shape[1]
    owner, core, owners = place[0], place[1], place[2]

    def piece(i):
        where = pl.ds(pl.multiple_of(i * rows, rows), rows)
        return pltpu.make_async_copy(matrix_hbm.at[where], matrix.at[where], sems.at[i])

    blocks_in = pltpu.make_async_copy(pattern_hbm, pattern, pattern_sem)
    blocks_in.start()
    first = pltpu.make_async_copy(start_hbm, fronts, start_sem)
    first.start()
    for i in range(AHEAD):
        piece(i).start()
    second[...] = jnp.full(second.shape, core.astype(F32))
    later = owner - order[...]
    later = jnp.where(later < 0, later + owners, later)
    turn[...] = later
    last = order[...] + (owners - 1)
    last = jnp.where(last >= owners, last - owners, last)
    apart[...] = last ^ owner
    batches, rows_in = narrow.shape[:2]
    batch = slices // batches
    narrow[:, batch:, :] = jnp.ones((batches, rows_in - batch, voxels), BF16)
    first.wait()
    chosen = [later[:, f : f + 1] == 0 for f in range(1, fronts.shape[0])]
    step = 4 * side

    @pl.loop(0, voxels // step)
    def _(i):
        cols = pl.ds(pl.multiple_of(i * step, step), step)
        got = fronts[0, :, cols].astype(F32)
        for f, here in enumerate(chosen):
            got = jnp.where(here, fronts[f + 1, :, cols].astype(F32), got)
        for b in range(batches):
            part = got[b * batch : (b + 1) * batch]
            volume[b, :, cols] = part
            narrow[b, :batch, cols] = part.astype(BF16)

    blocks_in.wait()

    @pl.loop(0, loads)
    def _(i):
        piece(i).wait()

        @pl.when(i + AHEAD < loads)
        def _():
            piece(i + AHEAD).start()

        where = pl.ds(pl.multiple_of(i * rows, rows), rows)
        for c in range(0, col_blocks, 2):
            cols = slice(c * side, (c + 2) * side)
            blocks = matrix[where, cols]
            masked = []
            for r in range(per_load):
                keep = [pattern[i * per_load + r, c + k].astype(F32).astype(BF16) for k in (0, 1)]
                part = blocks[r * side : (r + 1) * side]
                masked.append(
                    jnp.concatenate([part[:, :side] * keep[0], part[:, side:] * keep[1]], 1)
                )
            blocks = jnp.concatenate(masked, 0)
            matrix[where, cols] = blocks
            flipped[cols, where] = blocks.T


def project(place, volume, flipped, rays):
    count = rays.shape[1]
    step = min(count, 1024)
    offset = place[0] * count

    @pl.loop(0, count // step)
    def _(i):
        where = pl.ds(pl.multiple_of(offset + i * step, step), step)
        rays[:, pl.ds(pl.multiple_of(i * step, step), step)] = dot_nn(volume[...], flipped[:, where])


def added(one, two, before, total):
    total[...] = one[...] + two[...]


def scaled(total, target, inverse, before, residue):
    residue[...] = ((target[...] - total[...]) * inverse[...]).astype(BF16)


def spread_first(place, residue, matrix, spread):
    count = residue.shape[1]
    where = pl.ds(pl.multiple_of(place[0] * count, count), count)
    step = 2048

    @pl.loop(0, matrix.shape[1] // step)
    def _(c):
        cols = pl.ds(pl.multiple_of(c * step, step), step)
        spread[:, cols] = dot_nn(residue[...], matrix[where, cols])


def spread_last(first, place, residue, so_far, volume, column, matrix, out, *column_out):
    count = residue.shape[1]
    slices = out.shape[0]
    step = 2048
    where = pl.ds(pl.multiple_of(place[0] * count, count), count)

    @pl.loop(0, matrix.shape[1] // step)
    def _(c):
        cols = pl.ds(pl.multiple_of(c * step, step), step)
        total = so_far[:, cols] + dot_nn(residue[...], matrix[where, cols])
        if first:
            inverse = 1.0 / total[slices : slices + 1, :]
            column_out[0][:, cols] = inverse
        else:
            inverse = column[:, cols]
        out[:, cols] = volume[:, cols] + total[:slices] * inverse


def passed(x, axis, distance):
    size = lax.axis_size(axis)
    return lax.ppermute(x, axis, [(i, (i + distance) % size) for i in range(size)])


def swapped(x, axis, bit):
    size = lax.axis_size(axis)
    return lax.ppermute(x, axis, [(i, i ^ bit) for i in range(size)])


def after(value, token):
    return value if token is None else lax.optimization_barrier((value, token))[0]


def from_all_owners(block):
    owners = lax.axis_size("subset")
    if owners != 4:
        return [block] + [swapped(block, "subset", d) for d in range(1, owners)]
    half = block.shape[1] // 2
    near = swapped(block, "subset", 1)
    far = swapped(block, "subset", 2)
    both = [swapped(far[:, :half], "subset", 1), swapped(near[:, half:], "subset", 2)]
    return [block, near, far, jnp.concatenate(both, axis=1)]


def body(start_volume, measured, system_values, block_pattern, subset_order):
    owner = lax.axis_index("subset")
    owners = lax.axis_size("subset")
    core = lax.axis_index("tile") % 2
    tiles = lax.axis_size("tile")
    fronts, slices, voxels = start_volume.shape
    ray_count = measured.shape[-1]
    ray_blocks = block_pattern.shape[1]
    half = ray_count // 2
    batch = slices // BATCHES
    rows = batch + EXTRA
    passes = owners
    loads = ray_blocks // 2
    work = 2 * slices * ray_count * voxels
    place = jnp.stack([owner, core, jnp.int32(owners)]).astype(jnp.int32)
    own = jnp.reshape(core, (1,)).astype(jnp.int32)
    other = jnp.reshape(1 - core, (1,)).astype(jnp.int32)
    place, own, other = lax.optimization_barrier((place, own, other))

    def pick(turns, j, parts):
        got = parts[0]
        for f in range(1, fronts):
            got = jnp.where(turns[:, f : f + 1] == j, parts[f], got)
        return got

    hbm = pltpu.with_memory_space_constraint
    matrix, flipped, all_rows, volume, turn, apart, second = call(
        load_kernel,
        (
            pltpu.VMEM((ray_count, voxels), BF16),
            pltpu.VMEM((voxels, ray_count), BF16),
            shaped((BATCHES, rows, voxels), BF16),
            shaped((BATCHES, batch, voxels)),
            shaped((slices, fronts), jnp.int32),
            shaped((slices, fronts), jnp.int32),
            shaped((1, half)),
        ),
        (
            place, hbm(system_values[0], pltpu.HBM), hbm(block_pattern[0], pltpu.HBM),
            subset_order,
            hbm(start_volume, pltpu.HBM),
        ),
        [SM, HB, HB, VM, HB],
        work,
        "load",
        scratch=[
            pltpu.VMEM((fronts, slices, voxels), BF16),
            pltpu.SMEM(block_pattern.shape[1:], jnp.int32),
            pltpu.SemaphoreType.DMA((loads,)),
            pltpu.SemaphoreType.DMA,
            pltpu.SemaphoreType.DMA,
        ],
        vmem=10 << 20,
    )
    matrix = pltpu.with_memory_space_constraint(matrix, pltpu.VMEM)
    flipped = pltpu.with_memory_space_constraint(flipped, pltpu.VMEM)

    def products(kernel, shape, args, specs, name):
        return call(kernel, shape, args, specs, work // 2, name)

    targets = jnp.where(second == 0, measured[0][:, :, :half], measured[0][:, :, half:])
    these = [slice(n * batch, (n + 1) * batch) for n in range(BATCHES)]
    now = [volume[n] for n in range(BATCHES)]
    narrow = [all_rows[n] if n == 0 else all_rows[n, :batch] for n in range(BATCHES)]
    column = jnp.zeros((1, voxels), F32)
    inverse_row = None
    token = None
    for j in range(passes):
        totals = []
        for n in range(BATCHES):
            if j > 0:
                now[n] = after(now[n], token).astype(F32)
                narrow[n] = now[n].astype(BF16)
            height = narrow[n].shape[0]
            sent, held = [
                products(
                    project, shaped((height, half)), (where, narrow[n], flipped), [SM, VM, VM],
                    "project",
                )
                for where in (other, own)
            ]
            got = swapped((sent * RAY_SCALE).astype(F16), "tile", 1)
            totals.append(held * RAY_SCALE + got.astype(F32))
            token = totals[n].astype(F16)
        if j == 0:
            for n in range(BATCHES):
                bit = 2
                while bit < tiles:
                    got = swapped(totals[n].astype(F16), "tile", bit).astype(F32)
                    if n > 0 and bit == 2:
                        totals[n] = call(
                            added, shaped(got.shape), (totals[n], got, totals[n - 1]),
                            [VM, VM, AN], 1, "added",
                        )
                    else:
                        totals[n] = totals[n] + got
                    bit *= 2
            token = totals[-1].astype(F16)
        else:
            got = [
                [swapped(t.astype(F16), "tile", bits) for bits in range(2, tiles, 2)]
                for t in totals
            ]
            for n in range(BATCHES):
                for part in got[n]:
                    totals[n] = totals[n] + part.astype(F32)
                token = totals[n].astype(F16)
        for n in range(BATCHES):
            total = totals[n] if n == 0 else after(totals[n], token)
            sums = j == 0 and n == 0
            if sums:
                inverse_row = 1.0 / total[batch : batch + 1]
                total = total[:batch]
            target = pick(turn[these[n]], j, targets[:, these[n]].astype(F32)) * RAY_SCALE
            if n > 0 and j + 1 == passes:
                residue = call(
                    scaled, shaped((batch, half), BF16), (total, target, inverse_row, got[0]),
                    [VM, VM, VM, AN], 1, "scaled",
                )
            else:
                residue = ((target - total) * inverse_row).astype(BF16)
            if sums:
                residue = jnp.concatenate([residue, jnp.ones((EXTRA, half), BF16)])
            height = residue.shape[0]
            their_residue = swapped(residue, "tile", 1)
            spread = products(
                spread_first, shaped((height, voxels)), (own, residue, matrix),
                [SM, VM, VM], "spread_first",
            )
            shapes = [shaped((batch, voxels))]
            if sums:
                shapes.append(shaped((1, voxels)))
            got = products(
                functools.partial(spread_last, sums), tuple(shapes),
                (other, their_residue, spread, now[n], column, matrix),
                [SM, VM, VM, VM, VM, VM], "spread_last",
            )
            now[n] = got[0]
            if sums:
                column = got[1]
            token = now[n].astype(F16)
            if j + 1 < passes:
                now[n] = passed(token, "subset", 1)
    outs = []
    for n in range(BATCHES):
        found = from_all_owners(now[n].astype(BF16))
        parts = []
        for f in range(fronts):
            got = found[0]
            for d in range(1, owners):
                got = jnp.where(apart[these[n], f : f + 1] == d, found[d], got)
            parts.append(got)
        outs.append(jnp.stack(parts))
    return jnp.concatenate(outs, axis=1)


def solution(mesh):
    placed = (
        P(None, None, "tile"),
        P("subset", None, None, None),
        P("subset", None, "tile"),
        P("subset", None, "tile"),
        P(),
    )
    return jax.shard_map(
        body, mesh=mesh, in_specs=placed, out_specs=P(None, None, "tile"), check_vma=False
    )
```

```python
import functools

import jax
import jax.numpy as jnp
from jax import lax
from jax.experimental import pallas as pl
from jax.experimental.pallas import tpu as pltpu
from jax.sharding import PartitionSpec as P

F32, BF16, F16 = jnp.float32, jnp.bfloat16, jnp.float16
RAY_SCALE = 2.0**-14
EXTRA = 16
COST = 16
AHEAD = 2
BATCHES = 2
VM = pl.BlockSpec(memory_space=pltpu.VMEM)
SM = pl.BlockSpec(memory_space=pltpu.SMEM)
HB = pl.BlockSpec(memory_space=pltpu.HBM)
AN = pl.BlockSpec(memory_space=pl.ANY)


def call(kernel, out_shape, args, specs, flops, name, scratch=(), vmem=8 << 20):
    out_specs = jax.tree.map(lambda _: VM, out_shape)
    return pl.pallas_call(
        kernel,
        out_shape=out_shape,
        in_specs=specs,
        out_specs=out_specs,
        scratch_shapes=scratch,
        name=name,
        cost_estimate=pl.CostEstimate(
            flops=COST * flops, bytes_accessed=0, transcendentals=0
        ),
        compiler_params=pltpu.CompilerParams(vmem_limit_bytes=vmem),
    )(*args)


def shaped(shape, dtype=F32):
    return jax.ShapeDtypeStruct(shape, dtype)


def dot_nn(a, b):
    return lax.dot_general(a, b, (((1,), (0,)), ((), ())), preferred_element_type=F32)


def load_kernel(
    place, matrix_hbm, pattern_hbm, order, start_hbm, matrix, flipped, narrow, volume, turn, apart,
    second, fronts, pattern, ends_in, sems, start_sem, pattern_sem, order_sem,
):
    ray_blocks, col_blocks = pattern.shape
    ray_count, voxels = matrix.shape
    side = ray_count // ray_blocks
    loads = sems.shape[0]
    rows = ray_count // loads
    per_load = ray_blocks // loads
    slices = fronts.shape[1]
    owner, core, owners = place[0], place[1], place[2]

    def piece(i):
        where = pl.ds(pl.multiple_of(i * rows, rows), rows)
        return pltpu.make_async_copy(matrix_hbm.at[where], matrix.at[where], sems.at[i])

    order_in = pltpu.make_async_copy(order, ends_in, order_sem)
    order_in.start()
    blocks_in = pltpu.make_async_copy(pattern_hbm, pattern, pattern_sem)
    blocks_in.start()
    first = pltpu.make_async_copy(start_hbm, fronts, start_sem)
    first.start()
    for i in range(AHEAD):
        piece(i).start()
    second[...] = jnp.full(second.shape, core.astype(F32))
    order_in.wait()
    ends = jnp.transpose(ends_in[...])
    later = owner - ends
    later = jnp.where(later < 0, later + owners, later)
    turn[...] = later
    last = ends + (owners - 1)
    last = jnp.where(last >= owners, last - owners, last)
    apart[...] = last ^ owner
    batches, rows_in = narrow.shape[:2]
    batch = slices // batches
    narrow[:, batch:, :] = jnp.ones((batches, rows_in - batch, voxels), BF16)
    first.wait()
    chosen = [later[:, f : f + 1] == 0 for f in range(1, fronts.shape[0])]
    step = 4 * side

    @pl.loop(0, voxels // step)
    def _(i):
        cols = pl.ds(pl.multiple_of(i * step, step), step)
        got = fronts[0, :, cols].astype(F32)
        for f, here in enumerate(chosen):
            got = jnp.where(here, fronts[f + 1, :, cols].astype(F32), got)
        for b in range(batches):
            part = got[b * batch : (b + 1) * batch]
            volume[b, :, cols] = part
            narrow[b, :batch, cols] = part.astype(BF16)

    blocks_in.wait()

    @pl.loop(0, loads)
    def _(i):
        piece(i).wait()

        @pl.when(i + AHEAD < loads)
        def _():
            piece(i + AHEAD).start()

        where = pl.ds(pl.multiple_of(i * rows, rows), rows)
        for c in range(0, col_blocks, 2):
            cols = slice(c * side, (c + 2) * side)
            blocks = matrix[where, cols]
            masked = []
            for r in range(per_load):
                keep = [pattern[i * per_load + r, c + k].astype(F32).astype(BF16) for k in (0, 1)]
                part = blocks[r * side : (r + 1) * side]
                masked.append(
                    jnp.concatenate([part[:, :side] * keep[0], part[:, side:] * keep[1]], 1)
                )
            blocks = jnp.concatenate(masked, 0)
            matrix[where, cols] = blocks
            flipped[cols, where] = blocks.T


def project(place, volume, flipped, rays):
    count = rays.shape[1]
    step = min(count, 1024)
    offset = place[0] * count

    @pl.loop(0, count // step)
    def _(i):
        where = pl.ds(pl.multiple_of(offset + i * step, step), step)
        rays[:, pl.ds(pl.multiple_of(i * step, step), step)] = dot_nn(volume[...], flipped[:, where])


def added(one, two, before, total):
    total[...] = one[...] + two[...]


def scaled(total, target, inverse, before, residue):
    residue[...] = ((target[...] - total[...]) * inverse[...]).astype(BF16)


def spread_first(place, residue, matrix, spread):
    count = residue.shape[1]
    where = pl.ds(pl.multiple_of(place[0] * count, count), count)
    step = 2048

    @pl.loop(0, matrix.shape[1] // step)
    def _(c):
        cols = pl.ds(pl.multiple_of(c * step, step), step)
        spread[:, cols] = dot_nn(residue[...], matrix[where, cols])


def spread_last(first, place, residue, so_far, volume, column, matrix, out, *column_out):
    count = residue.shape[1]
    slices = out.shape[0]
    step = 2048
    where = pl.ds(pl.multiple_of(place[0] * count, count), count)

    @pl.loop(0, matrix.shape[1] // step)
    def _(c):
        cols = pl.ds(pl.multiple_of(c * step, step), step)
        total = so_far[:, cols] + dot_nn(residue[...], matrix[where, cols])
        if first:
            inverse = 1.0 / total[slices : slices + 1, :]
            column_out[0][:, cols] = inverse
        else:
            inverse = column[:, cols]
        out[:, cols] = volume[:, cols] + total[:slices] * inverse


def passed(x, axis, distance):
    size = lax.axis_size(axis)
    return lax.ppermute(x, axis, [(i, (i + distance) % size) for i in range(size)])


def swapped(x, axis, bit):
    size = lax.axis_size(axis)
    return lax.ppermute(x, axis, [(i, i ^ bit) for i in range(size)])


def after(value, token):
    return value if token is None else lax.optimization_barrier((value, token))[0]


def from_all_owners(block):
    owners = lax.axis_size("subset")
    if owners != 4:
        return [block] + [swapped(block, "subset", d) for d in range(1, owners)]
    half = block.shape[1] // 2
    near = swapped(block, "subset", 1)
    far = swapped(block, "subset", 2)
    both = [swapped(far[:, :half], "subset", 1), swapped(near[:, half:], "subset", 2)]
    return [block, near, far, jnp.concatenate(both, axis=1)]


def body(start_volume, measured, system_values, block_pattern, subset_order):
    owner = lax.axis_index("subset")
    owners = lax.axis_size("subset")
    core = lax.axis_index("tile") % 2
    tiles = lax.axis_size("tile")
    fronts, slices, voxels = start_volume.shape
    ray_count = measured.shape[-1]
    ray_blocks = block_pattern.shape[1]
    half = ray_count // 2
    batch = slices // BATCHES
    rows = batch + EXTRA
    passes = owners
    loads = ray_blocks // 2
    work = 2 * slices * ray_count * voxels
    place = jnp.stack([owner, core, jnp.int32(owners)]).astype(jnp.int32)
    own = jnp.reshape(core, (1,)).astype(jnp.int32)
    other = jnp.reshape(1 - core, (1,)).astype(jnp.int32)
    place, own, other = lax.optimization_barrier((place, own, other))

    def pick(turns, j, parts):
        got = parts[0]
        for f in range(1, fronts):
            got = jnp.where(turns[:, f : f + 1] == j, parts[f], got)
        return got

    hbm = pltpu.with_memory_space_constraint
    matrix, flipped, all_rows, volume, turn, apart, second = call(
        load_kernel,
        (
            pltpu.VMEM((ray_count, voxels), BF16),
            pltpu.VMEM((voxels, ray_count), BF16),
            shaped((BATCHES, rows, voxels), BF16),
            shaped((BATCHES, batch, voxels)),
            shaped((slices, fronts), jnp.int32),
            shaped((slices, fronts), jnp.int32),
            shaped((1, half)),
        ),
        (
            place, hbm(system_values[0], pltpu.HBM), hbm(block_pattern[0], pltpu.HBM),
            hbm(jnp.transpose(subset_order), pltpu.HBM),
            hbm(start_volume, pltpu.HBM),
        ),
        [SM, HB, HB, HB, HB],
        work,
        "load",
        scratch=[
            pltpu.VMEM((fronts, slices, voxels), BF16),
            pltpu.SMEM(block_pattern.shape[1:], jnp.int32),
            pltpu.VMEM((fronts, slices), jnp.int32),
            pltpu.SemaphoreType.DMA((loads,)),
            pltpu.SemaphoreType.DMA,
            pltpu.SemaphoreType.DMA,
            pltpu.SemaphoreType.DMA,
        ],
        vmem=10 << 20,
    )
    matrix = pltpu.with_memory_space_constraint(matrix, pltpu.VMEM)
    flipped = pltpu.with_memory_space_constraint(flipped, pltpu.VMEM)

    def products(kernel, shape, args, specs, name):
        return call(kernel, shape, args, specs, work // 2, name)

    targets = jnp.where(second == 0, measured[0][:, :, :half], measured[0][:, :, half:])
    these = [slice(n * batch, (n + 1) * batch) for n in range(BATCHES)]
    now = [volume[n] for n in range(BATCHES)]
    narrow = [all_rows[n] if n == 0 else all_rows[n, :batch] for n in range(BATCHES)]
    column = jnp.zeros((1, voxels), F32)
    inverse_row = None
    token = None
    for j in range(passes):
        totals = []
        for n in range(BATCHES):
            if j > 0:
                now[n] = after(now[n], token).astype(F32)
                narrow[n] = now[n].astype(BF16)
            height = narrow[n].shape[0]
            sent, held = [
                products(
                    project, shaped((height, half)), (where, narrow[n], flipped), [SM, VM, VM],
                    "project",
                )
                for where in (other, own)
            ]
            got = swapped((sent * RAY_SCALE).astype(F16), "tile", 1)
            totals.append(held * RAY_SCALE + got.astype(F32))
            token = totals[n].astype(F16)
        if j == 0:
            for n in range(BATCHES):
                bit = 2
                while bit < tiles:
                    got = swapped(totals[n].astype(F16), "tile", bit).astype(F32)
                    if n > 0 and bit == 2:
                        totals[n] = call(
                            added, shaped(got.shape), (totals[n], got, totals[n - 1]),
                            [VM, VM, AN], 1, "added",
                        )
                    else:
                        totals[n] = totals[n] + got
                    bit *= 2
            token = totals[-1].astype(F16)
        else:
            got = [
                [swapped(t.astype(F16), "tile", bits) for bits in range(2, tiles, 2)]
                for t in totals
            ]
            for n in range(BATCHES):
                for part in got[n]:
                    totals[n] = totals[n] + part.astype(F32)
                token = totals[n].astype(F16)
        for n in range(BATCHES):
            total = totals[n] if n == 0 else after(totals[n], token)
            sums = j == 0 and n == 0
            if sums:
                inverse_row = 1.0 / total[batch : batch + 1]
                total = total[:batch]
            target = pick(turn[these[n]], j, targets[:, these[n]].astype(F32)) * RAY_SCALE
            if n > 0 and j + 1 == passes:
                residue = call(
                    scaled, shaped((batch, half), BF16), (total, target, inverse_row, got[0]),
                    [VM, VM, VM, AN], 1, "scaled",
                )
            else:
                residue = ((target - total) * inverse_row).astype(BF16)
            if sums:
                residue = jnp.concatenate([residue, jnp.ones((EXTRA, half), BF16)])
            height = residue.shape[0]
            their_residue = swapped(residue, "tile", 1)
            spread = products(
                spread_first, shaped((height, voxels)), (own, residue, matrix),
                [SM, VM, VM], "spread_first",
            )
            shapes = [shaped((batch, voxels))]
            if sums:
                shapes.append(shaped((1, voxels)))
            got = products(
                functools.partial(spread_last, sums), tuple(shapes),
                (other, their_residue, spread, now[n], column, matrix),
                [SM, VM, VM, VM, VM, VM], "spread_last",
            )
            now[n] = got[0]
            if sums:
                column = got[1]
            token = now[n].astype(F16)
            if j + 1 < passes:
                now[n] = passed(token, "subset", 1)
    out = jnp.zeros(start_volume.shape, BF16)
    for n in range(BATCHES):
        found = from_all_owners(now[n].astype(BF16))
        parts = []
        for f in range(fronts):
            got = found[0]
            for d in range(1, owners):
                got = jnp.where(apart[these[n], f : f + 1] == d, found[d], got)
            parts.append(got)
        out = lax.dynamic_update_slice(out, jnp.stack(parts), (0, n * batch, 0))
    return out


def solution(mesh):
    placed = (
        P(None, None, "tile"),
        P("subset", None, None, None),
        P("subset", None, "tile"),
        P("subset", None, "tile"),
        P(),
    )
    return jax.shard_map(
        body, mesh=mesh, in_specs=placed, out_specs=P(None, None, "tile"), check_vma=False
    )
```

```python
import functools

import jax
import jax.numpy as jnp
from jax import lax
from jax.experimental import pallas as pl
from jax.experimental.pallas import tpu as pltpu
from jax.sharding import PartitionSpec as P

F32, BF16, F16 = jnp.float32, jnp.bfloat16, jnp.float16
RAY_SCALE = 2.0**-14
EXTRA = 16
COST = 16
AHEAD = 2
BATCHES = 2
VM = pl.BlockSpec(memory_space=pltpu.VMEM)
SM = pl.BlockSpec(memory_space=pltpu.SMEM)
HB = pl.BlockSpec(memory_space=pltpu.HBM)
AN = pl.BlockSpec(memory_space=pl.ANY)


def call(kernel, out_shape, args, specs, flops, name, scratch=(), vmem=8 << 20):
    out_specs = jax.tree.map(lambda _: VM, out_shape)
    return pl.pallas_call(
        kernel,
        out_shape=out_shape,
        in_specs=specs,
        out_specs=out_specs,
        scratch_shapes=scratch,
        name=name,
        cost_estimate=pl.CostEstimate(
            flops=COST * flops, bytes_accessed=0, transcendentals=0
        ),
        compiler_params=pltpu.CompilerParams(vmem_limit_bytes=vmem),
    )(*args)


def shaped(shape, dtype=F32):
    return jax.ShapeDtypeStruct(shape, dtype)


def dot_nn(a, b):
    return lax.dot_general(a, b, (((1,), (0,)), ((), ())), preferred_element_type=F32)


def load_kernel(
    place, matrix_hbm, pattern_hbm, order, start_hbm, matrix, flipped, narrow, volume, turn, apart,
    second, fronts, pattern, ends_in, sems, start_sem, pattern_sem, order_sem,
):
    ray_blocks, col_blocks = pattern.shape
    ray_count, voxels = matrix.shape
    side = ray_count // ray_blocks
    loads = sems.shape[0]
    rows = ray_count // loads
    per_load = ray_blocks // loads
    slices = fronts.shape[1]
    owner, core, owners = place[0], place[1], place[2]

    def piece(i):
        where = pl.ds(pl.multiple_of(i * rows, rows), rows)
        return pltpu.make_async_copy(matrix_hbm.at[where], matrix.at[where], sems.at[i])

    order_in = pltpu.make_async_copy(order, ends_in, order_sem)
    order_in.start()
    blocks_in = pltpu.make_async_copy(pattern_hbm, pattern, pattern_sem)
    blocks_in.start()
    first = pltpu.make_async_copy(start_hbm, fronts, start_sem)
    first.start()
    for i in range(AHEAD):
        piece(i).start()
    second[...] = jnp.full(second.shape, core.astype(F32))
    order_in.wait()
    ends = jnp.transpose(ends_in[...])
    later = owner - ends
    later = jnp.where(later < 0, later + owners, later)
    turn[...] = later
    last = ends + (owners - 1)
    last = jnp.where(last >= owners, last - owners, last)
    apart[...] = last ^ owner
    batches, rows_in = narrow.shape[:2]
    batch = slices // batches
    narrow[:, batch:, :] = jnp.ones((batches, rows_in - batch, voxels), BF16)
    first.wait()
    chosen = [later[:, f : f + 1] == 0 for f in range(1, fronts.shape[0])]
    step = voxels // loads
    blocks_in.wait()

    @pl.loop(0, loads)
    def _(i):
        piece(i).wait()

        @pl.when(i + AHEAD < loads)
        def _():
            piece(i + AHEAD).start()

        cols = pl.ds(pl.multiple_of(i * step, step), step)
        got = fronts[0, :, cols].astype(F32)
        for f, here in enumerate(chosen):
            got = jnp.where(here, fronts[f + 1, :, cols].astype(F32), got)
        for b in range(batches):
            part = got[b * batch : (b + 1) * batch]
            volume[b, :, cols] = part
            narrow[b, :batch, cols] = part.astype(BF16)
        where = pl.ds(pl.multiple_of(i * rows, rows), rows)
        for c in range(0, col_blocks, 2):
            cols = slice(c * side, (c + 2) * side)
            blocks = matrix[where, cols]
            masked = []
            for r in range(per_load):
                keep = [pattern[i * per_load + r, c + k].astype(F32).astype(BF16) for k in (0, 1)]
                part = blocks[r * side : (r + 1) * side]
                masked.append(
                    jnp.concatenate([part[:, :side] * keep[0], part[:, side:] * keep[1]], 1)
                )
            blocks = jnp.concatenate(masked, 0)
            matrix[where, cols] = blocks
            flipped[cols, where] = blocks.T


def project(place, volume, flipped, rays):
    count = rays.shape[1]
    step = min(count, 1024)
    offset = place[0] * count

    @pl.loop(0, count // step)
    def _(i):
        where = pl.ds(pl.multiple_of(offset + i * step, step), step)
        rays[:, pl.ds(pl.multiple_of(i * step, step), step)] = dot_nn(volume[...], flipped[:, where])


def added(one, two, before, total):
    total[...] = one[...] + two[...]


def scaled(total, target, inverse, before, residue):
    residue[...] = ((target[...] - total[...]) * inverse[...]).astype(BF16)


def spread_first(place, residue, matrix, spread):
    count = residue.shape[1]
    where = pl.ds(pl.multiple_of(place[0] * count, count), count)
    step = 2048

    @pl.loop(0, matrix.shape[1] // step)
    def _(c):
        cols = pl.ds(pl.multiple_of(c * step, step), step)
        spread[:, cols] = dot_nn(residue[...], matrix[where, cols])


def spread_last(first, place, residue, so_far, volume, column, matrix, out, *column_out):
    count = residue.shape[1]
    slices = out.shape[0]
    step = 2048
    where = pl.ds(pl.multiple_of(place[0] * count, count), count)

    @pl.loop(0, matrix.shape[1] // step)
    def _(c):
        cols = pl.ds(pl.multiple_of(c * step, step), step)
        total = so_far[:, cols] + dot_nn(residue[...], matrix[where, cols])
        if first:
            inverse = 1.0 / total[slices : slices + 1, :]
            column_out[0][:, cols] = inverse
        else:
            inverse = column[:, cols]
        out[:, cols] = volume[:, cols] + total[:slices] * inverse


def passed(x, axis, distance):
    size = lax.axis_size(axis)
    return lax.ppermute(x, axis, [(i, (i + distance) % size) for i in range(size)])


def swapped(x, axis, bit):
    size = lax.axis_size(axis)
    return lax.ppermute(x, axis, [(i, i ^ bit) for i in range(size)])


def after(value, token):
    return value if token is None else lax.optimization_barrier((value, token))[0]


def from_all_owners(block):
    owners = lax.axis_size("subset")
    if owners != 4:
        return [block] + [swapped(block, "subset", d) for d in range(1, owners)]
    half = block.shape[1] // 2
    near = swapped(block, "subset", 1)
    far = swapped(block, "subset", 2)
    both = [swapped(far[:, :half], "subset", 1), swapped(near[:, half:], "subset", 2)]
    return [block, near, far, jnp.concatenate(both, axis=1)]


def body(start_volume, measured, system_values, block_pattern, subset_order):
    owner = lax.axis_index("subset")
    owners = lax.axis_size("subset")
    core = lax.axis_index("tile") % 2
    tiles = lax.axis_size("tile")
    fronts, slices, voxels = start_volume.shape
    ray_count = measured.shape[-1]
    ray_blocks = block_pattern.shape[1]
    half = ray_count // 2
    batch = slices // BATCHES
    rows = batch + EXTRA
    passes = owners
    loads = ray_blocks // 2
    work = 2 * slices * ray_count * voxels
    place = jnp.stack([owner, core, jnp.int32(owners)]).astype(jnp.int32)
    own = jnp.reshape(core, (1,)).astype(jnp.int32)
    other = jnp.reshape(1 - core, (1,)).astype(jnp.int32)
    place, own, other = lax.optimization_barrier((place, own, other))

    def pick(turns, j, parts):
        got = parts[0]
        for f in range(1, fronts):
            got = jnp.where(turns[:, f : f + 1] == j, parts[f], got)
        return got

    hbm = pltpu.with_memory_space_constraint
    matrix, flipped, all_rows, volume, turn, apart, second = call(
        load_kernel,
        (
            pltpu.VMEM((ray_count, voxels), BF16),
            pltpu.VMEM((voxels, ray_count), BF16),
            shaped((BATCHES, rows, voxels), BF16),
            shaped((BATCHES, batch, voxels)),
            shaped((slices, fronts), jnp.int32),
            shaped((slices, fronts), jnp.int32),
            shaped((1, half)),
        ),
        (
            place, hbm(system_values[0], pltpu.HBM), hbm(block_pattern[0], pltpu.HBM),
            hbm(jnp.transpose(subset_order), pltpu.HBM),
            hbm(start_volume, pltpu.HBM),
        ),
        [SM, HB, HB, HB, HB],
        work,
        "load",
        scratch=[
            pltpu.VMEM((fronts, slices, voxels), BF16),
            pltpu.SMEM(block_pattern.shape[1:], jnp.int32),
            pltpu.VMEM((fronts, slices), jnp.int32),
            pltpu.SemaphoreType.DMA((loads,)),
            pltpu.SemaphoreType.DMA,
            pltpu.SemaphoreType.DMA,
            pltpu.SemaphoreType.DMA,
        ],
        vmem=10 << 20,
    )
    matrix = pltpu.with_memory_space_constraint(matrix, pltpu.VMEM)
    flipped = pltpu.with_memory_space_constraint(flipped, pltpu.VMEM)

    def products(kernel, shape, args, specs, name):
        return call(kernel, shape, args, specs, work // 2, name)

    targets = jnp.where(second == 0, measured[0][:, :, :half], measured[0][:, :, half:])
    these = [slice(n * batch, (n + 1) * batch) for n in range(BATCHES)]
    now = [volume[n] for n in range(BATCHES)]
    narrow = [all_rows[n] if n == 0 else all_rows[n, :batch] for n in range(BATCHES)]
    column = jnp.zeros((1, voxels), F32)
    inverse_row = None
    token = None
    for j in range(passes):
        totals = []
        for n in range(BATCHES):
            if j > 0:
                now[n] = after(now[n], token).astype(F32)
                narrow[n] = now[n].astype(BF16)
            height = narrow[n].shape[0]
            sent, held = [
                products(
                    project, shaped((height, half)), (where, narrow[n], flipped), [SM, VM, VM],
                    "project",
                )
                for where in (other, own)
            ]
            got = swapped((sent * RAY_SCALE).astype(F16), "tile", 1)
            totals.append(held * RAY_SCALE + got.astype(F32))
            token = totals[n].astype(F16)
        if j == 0:
            for n in range(BATCHES):
                bit = 2
                while bit < tiles:
                    got = swapped(totals[n].astype(F16), "tile", bit).astype(F32)
                    if n > 0 and bit == 2:
                        totals[n] = call(
                            added, shaped(got.shape), (totals[n], got, totals[n - 1]),
                            [VM, VM, AN], 1, "added",
                        )
                    else:
                        totals[n] = totals[n] + got
                    bit *= 2
            token = totals[-1].astype(F16)
        else:
            got = [
                [swapped(t.astype(F16), "tile", bits) for bits in range(2, tiles, 2)]
                for t in totals
            ]
            for n in range(BATCHES):
                for part in got[n]:
                    totals[n] = totals[n] + part.astype(F32)
                token = totals[n].astype(F16)
        for n in range(BATCHES):
            total = totals[n] if n == 0 else after(totals[n], token)
            sums = j == 0 and n == 0
            if sums:
                inverse_row = 1.0 / total[batch : batch + 1]
                total = total[:batch]
            target = pick(turn[these[n]], j, targets[:, these[n]].astype(F32)) * RAY_SCALE
            if n > 0 and j + 1 == passes:
                residue = call(
                    scaled, shaped((batch, half), BF16), (total, target, inverse_row, got[0]),
                    [VM, VM, VM, AN], 1, "scaled",
                )
            else:
                residue = ((target - total) * inverse_row).astype(BF16)
            if sums:
                residue = jnp.concatenate([residue, jnp.ones((EXTRA, half), BF16)])
            height = residue.shape[0]
            their_residue = swapped(residue, "tile", 1)
            spread = products(
                spread_first, shaped((height, voxels)), (own, residue, matrix),
                [SM, VM, VM], "spread_first",
            )
            shapes = [shaped((batch, voxels))]
            if sums:
                shapes.append(shaped((1, voxels)))
            got = products(
                functools.partial(spread_last, sums), tuple(shapes),
                (other, their_residue, spread, now[n], column, matrix),
                [SM, VM, VM, VM, VM, VM], "spread_last",
            )
            now[n] = got[0]
            if sums:
                column = got[1]
            token = now[n].astype(F16)
            if j + 1 < passes:
                now[n] = passed(token, "subset", 1)
    out = jnp.zeros(start_volume.shape, BF16)
    for n in range(BATCHES):
        found = from_all_owners(now[n].astype(BF16))
        parts = []
        for f in range(fronts):
            got = found[0]
            for d in range(1, owners):
                got = jnp.where(apart[these[n], f : f + 1] == d, found[d], got)
            parts.append(got)
        out = lax.dynamic_update_slice(out, jnp.stack(parts), (0, n * batch, 0))
    return out


def solution(mesh):
    placed = (
        P(None, None, "tile"),
        P("subset", None, None, None),
        P("subset", None, "tile"),
        P("subset", None, "tile"),
        P(),
    )
    return jax.shard_map(
        body, mesh=mesh, in_specs=placed, out_specs=P(None, None, "tile"), check_vma=False
    )
```

```python
import functools

import jax
import jax.numpy as jnp
from jax import lax
from jax.experimental import pallas as pl
from jax.experimental.pallas import tpu as pltpu
from jax.sharding import PartitionSpec as P

F32, BF16, F16 = jnp.float32, jnp.bfloat16, jnp.float16
RAY_SCALE = 2.0**-14
EXTRA = 16
COST = 16
AHEAD = 2
BATCHES = 2
VM = pl.BlockSpec(memory_space=pltpu.VMEM)
SM = pl.BlockSpec(memory_space=pltpu.SMEM)
HB = pl.BlockSpec(memory_space=pltpu.HBM)
AN = pl.BlockSpec(memory_space=pl.ANY)


def call(kernel, out_shape, args, specs, flops, name, scratch=(), vmem=8 << 20):
    out_specs = jax.tree.map(lambda _: VM, out_shape)
    return pl.pallas_call(
        kernel,
        out_shape=out_shape,
        in_specs=specs,
        out_specs=out_specs,
        scratch_shapes=scratch,
        name=name,
        cost_estimate=pl.CostEstimate(
            flops=COST * flops, bytes_accessed=0, transcendentals=0
        ),
        compiler_params=pltpu.CompilerParams(vmem_limit_bytes=vmem),
    )(*args)


def shaped(shape, dtype=F32):
    return jax.ShapeDtypeStruct(shape, dtype)


def dot_nn(a, b):
    return lax.dot_general(a, b, (((1,), (0,)), ((), ())), preferred_element_type=F32)


def load_kernel(
    place, matrix_hbm, pattern_hbm, order, start_hbm, matrix, flipped, narrow, volume, turn, apart,
    second, fronts, pattern, ends_in, sems, start_sem, pattern_sem, order_sem,
):
    ray_blocks, col_blocks = pattern.shape
    ray_count, voxels = matrix.shape
    side = ray_count // ray_blocks
    loads = sems.shape[0]
    rows = ray_count // loads
    per_load = ray_blocks // loads
    slices = fronts.shape[1]
    owner, core, owners = place[0], place[1], place[2]

    def piece(i):
        where = pl.ds(pl.multiple_of(i * rows, rows), rows)
        return pltpu.make_async_copy(matrix_hbm.at[where], matrix.at[where], sems.at[i])

    order_in = pltpu.make_async_copy(order, ends_in, order_sem)
    order_in.start()
    blocks_in = pltpu.make_async_copy(pattern_hbm, pattern, pattern_sem)
    blocks_in.start()
    first = pltpu.make_async_copy(start_hbm, fronts, start_sem)
    first.start()
    for i in range(AHEAD):
        piece(i).start()
    second[...] = jnp.full(second.shape, core.astype(F32))
    order_in.wait()
    ends = jnp.transpose(ends_in[...])
    later = owner - ends
    later = jnp.where(later < 0, later + owners, later)
    turn[...] = later
    last = ends + (owners - 1)
    last = jnp.where(last >= owners, last - owners, last)
    apart[...] = last ^ owner
    batches, rows_in = narrow.shape[:2]
    batch = slices // batches
    narrow[:, batch:, :] = jnp.ones((batches, rows_in - batch, voxels), BF16)
    first.wait()
    chosen = [later[:, f : f + 1] == 0 for f in range(1, fronts.shape[0])]
    step = voxels // loads
    blocks_in.wait()

    @pl.loop(0, loads)
    def _(i):
        piece(i).wait()

        @pl.when(i + AHEAD < loads)
        def _():
            piece(i + AHEAD).start()

        cols = pl.ds(pl.multiple_of(i * step, step), step)
        got = fronts[0, :, cols].astype(F32)
        for f, here in enumerate(chosen):
            got = jnp.where(here, fronts[f + 1, :, cols].astype(F32), got)
        for b in range(batches):
            part = got[b * batch : (b + 1) * batch]
            volume[b, :, cols] = part
            narrow[b, :batch, cols] = part.astype(BF16)
        where = pl.ds(pl.multiple_of(i * rows, rows), rows)
        for c in range(0, col_blocks, 2):
            cols = slice(c * side, (c + 2) * side)
            blocks = matrix[where, cols]
            masked = []
            for r in range(per_load):
                keep = [pattern[i * per_load + r, c + k].astype(F32).astype(BF16) for k in (0, 1)]
                part = blocks[r * side : (r + 1) * side]
                masked.append(
                    jnp.concatenate([part[:, :side] * keep[0], part[:, side:] * keep[1]], 1)
                )
            blocks = jnp.concatenate(masked, 0)
            matrix[where, cols] = blocks
            flipped[cols, where] = blocks.T


def project(place, volume, flipped, rays):
    count = rays.shape[1]
    step = min(count, 1024)
    offset = place[0] * count

    @pl.loop(0, count // step)
    def _(i):
        where = pl.ds(pl.multiple_of(offset + i * step, step), step)
        rays[:, pl.ds(pl.multiple_of(i * step, step), step)] = dot_nn(volume[...], flipped[:, where])


def added(one, two, before, total):
    total[...] = one[...] + two[...]


def scaled(total, target, inverse, before, residue):
    residue[...] = ((target[...] - total[...]) * inverse[...]).astype(BF16)


def spread_first(parts, place, residue, matrix, spread):
    count = residue.shape[1]
    where = pl.ds(pl.multiple_of(place[0] * count, count), count)
    step = matrix.shape[1] // parts

    @pl.loop(0, matrix.shape[1] // step)
    def _(c):
        cols = pl.ds(pl.multiple_of(c * step, step), step)
        spread[:, cols] = dot_nn(residue[...], matrix[where, cols])


def spread_last(first, place, residue, so_far, volume, column, matrix, out, *column_out):
    count = residue.shape[1]
    slices = out.shape[0]
    step = matrix.shape[1] // 2
    where = pl.ds(pl.multiple_of(place[0] * count, count), count)

    @pl.loop(0, matrix.shape[1] // step)
    def _(c):
        cols = pl.ds(pl.multiple_of(c * step, step), step)
        total = so_far[:, cols] + dot_nn(residue[...], matrix[where, cols])
        if first:
            inverse = 1.0 / total[slices : slices + 1, :]
            column_out[0][:, cols] = inverse
        else:
            inverse = column[:, cols]
        out[:, cols] = volume[:, cols] + total[:slices] * inverse


def passed(x, axis, distance):
    size = lax.axis_size(axis)
    return lax.ppermute(x, axis, [(i, (i + distance) % size) for i in range(size)])


def swapped(x, axis, bit):
    size = lax.axis_size(axis)
    return lax.ppermute(x, axis, [(i, i ^ bit) for i in range(size)])


def after(value, token):
    return value if token is None else lax.optimization_barrier((value, token))[0]


def from_all_owners(block):
    owners = lax.axis_size("subset")
    if owners != 4:
        return [block] + [swapped(block, "subset", d) for d in range(1, owners)]
    half = block.shape[1] // 2
    near = swapped(block, "subset", 1)
    far = swapped(block, "subset", 2)
    both = [swapped(far[:, :half], "subset", 1), swapped(near[:, half:], "subset", 2)]
    return [block, near, far, jnp.concatenate(both, axis=1)]


def body(start_volume, measured, system_values, block_pattern, subset_order):
    owner = lax.axis_index("subset")
    owners = lax.axis_size("subset")
    core = lax.axis_index("tile") % 2
    tiles = lax.axis_size("tile")
    fronts, slices, voxels = start_volume.shape
    ray_count = measured.shape[-1]
    ray_blocks = block_pattern.shape[1]
    half = ray_count // 2
    batch = slices // BATCHES
    rows = batch + EXTRA
    passes = owners
    loads = ray_blocks // 2
    work = 2 * slices * ray_count * voxels
    place = jnp.stack([owner, core, jnp.int32(owners)]).astype(jnp.int32)
    own = jnp.reshape(core, (1,)).astype(jnp.int32)
    other = jnp.reshape(1 - core, (1,)).astype(jnp.int32)
    place, own, other = lax.optimization_barrier((place, own, other))

    def pick(turns, j, parts):
        got = parts[0]
        for f in range(1, fronts):
            got = jnp.where(turns[:, f : f + 1] == j, parts[f], got)
        return got

    hbm = pltpu.with_memory_space_constraint
    matrix, flipped, all_rows, volume, turn, apart, second = call(
        load_kernel,
        (
            pltpu.VMEM((ray_count, voxels), BF16),
            pltpu.VMEM((voxels, ray_count), BF16),
            shaped((BATCHES, rows, voxels), BF16),
            shaped((BATCHES, batch, voxels)),
            shaped((slices, fronts), jnp.int32),
            shaped((slices, fronts), jnp.int32),
            shaped((1, half)),
        ),
        (
            place, hbm(system_values[0], pltpu.HBM), hbm(block_pattern[0], pltpu.HBM),
            hbm(jnp.transpose(subset_order), pltpu.HBM),
            hbm(start_volume, pltpu.HBM),
        ),
        [SM, HB, HB, HB, HB],
        work,
        "load",
        scratch=[
            pltpu.VMEM((fronts, slices, voxels), BF16),
            pltpu.SMEM(block_pattern.shape[1:], jnp.int32),
            pltpu.VMEM((fronts, slices), jnp.int32),
            pltpu.SemaphoreType.DMA((loads,)),
            pltpu.SemaphoreType.DMA,
            pltpu.SemaphoreType.DMA,
            pltpu.SemaphoreType.DMA,
        ],
        vmem=10 << 20,
    )
    matrix = pltpu.with_memory_space_constraint(matrix, pltpu.VMEM)
    flipped = pltpu.with_memory_space_constraint(flipped, pltpu.VMEM)

    def products(kernel, shape, args, specs, name):
        return call(kernel, shape, args, specs, work // 2, name)

    targets = jnp.where(second == 0, measured[0][:, :, :half], measured[0][:, :, half:])
    these = [slice(n * batch, (n + 1) * batch) for n in range(BATCHES)]
    now = [volume[n] for n in range(BATCHES)]
    narrow = [all_rows[n] if n == 0 else all_rows[n, :batch] for n in range(BATCHES)]
    column = jnp.zeros((1, voxels), F32)
    inverse_row = None
    token = None
    for j in range(passes):
        totals = []
        for n in range(BATCHES):
            if j > 0:
                now[n] = after(now[n], token).astype(F32)
                narrow[n] = now[n].astype(BF16)
            height = narrow[n].shape[0]
            sent, held = [
                products(
                    project, shaped((height, half)), (where, narrow[n], flipped), [SM, VM, VM],
                    "project",
                )
                for where in (other, own)
            ]
            got = swapped((sent * RAY_SCALE).astype(F16), "tile", 1)
            totals.append(held * RAY_SCALE + got.astype(F32))
            token = totals[n].astype(F16)
        if j == 0:
            for n in range(BATCHES):
                bit = 2
                while bit < tiles:
                    got = swapped(totals[n].astype(F16), "tile", bit).astype(F32)
                    if n > 0 and bit == 2:
                        totals[n] = call(
                            added, shaped(got.shape), (totals[n], got, totals[n - 1]),
                            [VM, VM, AN], 1, "added",
                        )
                    else:
                        totals[n] = totals[n] + got
                    bit *= 2
            token = totals[-1].astype(F16)
        else:
            got = [
                [swapped(t.astype(F16), "tile", bits) for bits in range(2, tiles, 2)]
                for t in totals
            ]
            for n in range(BATCHES):
                for part in got[n]:
                    totals[n] = totals[n] + part.astype(F32)
                token = totals[n].astype(F16)
        for n in range(BATCHES):
            total = totals[n] if n == 0 else after(totals[n], token)
            sums = j == 0 and n == 0
            if sums:
                inverse_row = 1.0 / total[batch : batch + 1]
                total = total[:batch]
            target = pick(turn[these[n]], j, targets[:, these[n]].astype(F32)) * RAY_SCALE
            if n > 0 and j + 1 == passes:
                residue = call(
                    scaled, shaped((batch, half), BF16), (total, target, inverse_row, got[0]),
                    [VM, VM, VM, AN], 1, "scaled",
                )
            else:
                residue = ((target - total) * inverse_row).astype(BF16)
            if sums:
                residue = jnp.concatenate([residue, jnp.ones((EXTRA, half), BF16)])
            height = residue.shape[0]
            their_residue = swapped(residue, "tile", 1)
            spread = products(
                functools.partial(spread_first, 1 if 0 < j < 3 else 2), shaped((height, voxels)), (own, residue, matrix),
                [SM, VM, VM], "spread_first",
            )
            shapes = [shaped((batch, voxels))]
            if sums:
                shapes.append(shaped((1, voxels)))
            got = products(
                functools.partial(spread_last, sums), tuple(shapes),
                (other, their_residue, spread, now[n], column, matrix),
                [SM, VM, VM, VM, VM, VM], "spread_last",
            )
            now[n] = got[0]
            if sums:
                column = got[1]
            token = now[n].astype(F16)
            if j + 1 < passes:
                now[n] = passed(token, "subset", 1)
    out = jnp.zeros(start_volume.shape, BF16)
    for n in range(BATCHES):
        found = from_all_owners(now[n].astype(BF16))
        parts = []
        for f in range(fronts):
            got = found[0]
            for d in range(1, owners):
                got = jnp.where(apart[these[n], f : f + 1] == d, found[d], got)
            parts.append(got)
        out = lax.dynamic_update_slice(out, jnp.stack(parts), (0, n * batch, 0))
    return out


def solution(mesh):
    placed = (
        P(None, None, "tile"),
        P("subset", None, None, None),
        P("subset", None, "tile"),
        P("subset", None, "tile"),
        P(),
    )
    return jax.shard_map(
        body, mesh=mesh, in_specs=placed, out_specs=P(None, None, "tile"), check_vma=False
    )
```
